32 devices in a mesh: samp: 2 (over x), feat: 16 (over z, y, core).
Axes of the slice: x: 2, y: 2, z: 4, core: 2. Of those that a mesh axis runs over, the one named last changes fastest.
Arguments:
- embeddings: bfloat16 [2048, 1024], P('samp'), may hold values from -6 to 6
- frequencies: bfloat16 [1024, 8192], P(None, 'feat'), may hold values from -0.1875 to 0.1875
- phases: float32 [8192], P('feat'), may hold values from -3.140625 to 3.140625
- treat_freq: float32 [8192], P('feat'), may hold values from -3.140625 to 3.140625
- treatment: int32 [2048], P('samp'), may hold values from 0 to 1
- flips: int32 [2048], P('samp'), may hold values from 0 to 1
- panel: int32 [1], replicated, may hold values from 0 to 15
Outputs:
- schur: float32 [8192, 8192], P('samp', 'feat')
- panel_factor: float32 [8192, 512], P('samp')
- moment_scaled: float32 [8192], P('feat')
The draws below stay inside these ranges and needn't reach their ends.
All inputs are finite; a program needn't handle non-finite values.
Results may differ from the reference program's by a relative error of at most 0.0032.
Values may be sent and summed in bfloat16 or wider, within the bound.
A program may use at most 128 MiB of HBM per device.

```python
import jax
import jax.numpy as jnp
from jax import lax

EMB = 1024
FEATS = 8192
PANEL = 512
IMPS = 2048


def plant(array, own_key, smallest, top_value):
    shape = array.shape
    index_at = [jax.random.randint(jax.random.fold_in(own_key, axis), (), 0, shape[axis]) for axis in range(len(shape))]
    array = array.at[tuple(index_at)].set(smallest)
    longest = shape.index(max(shape))
    index_at[longest] = (index_at[longest] + 1) % shape[longest]
    return array.at[tuple(index_at)].set(top_value)


def level_of(own_key, shape, shards, least, high):
    def one(axis_at, blocks):
        steps = jax.random.uniform(jax.random.fold_in(jax.random.fold_in(own_key, 6), axis_at), (blocks,), jnp.float32, least / len(shards), high / len(shards))
        return jnp.repeat(jnp.exp(steps), shape[axis_at] // blocks).reshape((-1,) + (1,) * (len(shape) - axis_at - 1))

    gain = one(*shards[0])
    for cut in shards[1:]:
        gain = gain * one(*cut)
    return gain


def normal_values(own_key, shape, spread, bound, cuts=(), held_as=jnp.bfloat16):
    level = level_of(own_key, shape, cuts, -0.22, 0.18) if cuts else 1.0
    array = jax.random.normal(own_key, shape, jnp.float32) * spread * level
    return jnp.minimum(jnp.maximum(array, -bound), bound).astype(held_as)


def setup_inputs(seed: int = 0) -> dict:
    key_of = jax.random.split(jax.random.key(seed), 8)
    embeddings = normal_values(key_of[0], (IMPS, EMB), 1.0, 6.0, ((0, 2),))
    frequencies = normal_values(key_of[1], (EMB, FEATS), EMB ** -0.5, 0.1875, ((1, 16),))
    phases = jnp.clip(jax.random.uniform(key_of[2], (FEATS,), jnp.float32, -3.140625, 3.140625), -3.140625, 3.140625)
    treat_freq = jnp.clip(jax.random.uniform(key_of[3], (FEATS,), jnp.float32, -3.140625, 3.140625), -3.140625, 3.140625)
    treatment = plant(jax.random.randint(key_of[4], (IMPS,), 0, 2), jax.random.fold_in(key_of[4], 1), 0, 1).astype(jnp.int32)
    flips = plant(jax.random.randint(key_of[5], (IMPS,), 0, 2), jax.random.fold_in(key_of[5], 1), 0, 1).astype(jnp.int32)
    panel = jax.random.randint(key_of[6], (1,), 0, FEATS // PANEL).astype(jnp.int32)
    return {"embeddings": embeddings, "frequencies": frequencies, "phases": phases, "treat_freq": treat_freq, "treatment": treatment, "flips": flips, "panel": panel}


ridge = 0.1
root_two = 1.4142135623730951

def cosine_map(project, phases, treat_freq, treated):
    return root_two * jnp.cos(project + phases[None, :] + treated[:, None] * treat_freq[None, :])

def reference(embeddings, frequencies, phases, treat_freq, treatment, flips, panel):
    project = jnp.dot(embeddings.astype(jnp.float32), frequencies.astype(jnp.float32), preferred_element_type=jnp.float32)
    treated = treatment.astype(jnp.float32)
    flipped = flips.astype(jnp.float32)
    counter = treated + flipped - 2.0 * treated * flipped
    observed = cosine_map(project, phases, treat_freq, treated)
    counterfactual = cosine_map(project, phases, treat_freq, counter)
    features = observed.astype(jnp.bfloat16).astype(jnp.float32)
    sample_count = embeddings.shape[0]
    gram = jnp.dot(features.T.astype(jnp.float32), features.astype(jnp.float32), precision=lax.Precision.HIGHEST, preferred_element_type=jnp.float32) / sample_count
    gram = gram + ridge * jnp.eye(FEATS, dtype=jnp.float32)
    moment = lax.optimization_barrier(jnp.sum(counterfactual - observed, axis=0)) / sample_count
    first_col = (panel[0] * PANEL).astype(jnp.int32)
    panel_cols = lax.dynamic_slice_in_dim(gram, first_col, PANEL, 1)
    pivot = lax.dynamic_slice_in_dim(panel_cols, first_col, PANEL, 0)
    lower = jnp.linalg.cholesky(pivot)
    factor_t = lax.linalg.triangular_solve(lower, panel_cols.T, left_side=True, lower=True)
    panel_factor = factor_t.T
    schur = gram - jnp.dot(panel_factor, factor_t, precision=lax.Precision.HIGHEST)
    moment_panel = lax.dynamic_slice_in_dim(moment, first_col, PANEL, 0)
    solved = lax.linalg.triangular_solve(lower, moment_panel[:, None], left_side=True, lower=True)[:, 0]
    reduced = moment - jnp.dot(panel_factor, solved, precision=lax.Precision.HIGHEST)
    return (schur, panel_factor, jnp.sqrt(jnp.float32(sample_count)) * reduced)
```

```python
import functools

import jax
import jax.numpy as jnp
from jax import lax
from jax.experimental import pallas as pl
from jax.experimental.pallas import tpu as pltpu
from jax.sharding import PartitionSpec as P

PANEL = 512
TILE = 128
LANES = 128

ridge = 0.1
turn = 0.15915494309189535
magic = 12582912.0
VMEM_BYTES = 58 * 1024 * 1024
COS = (1.4142124462507522, -27.915133726537626, 91.8229879115028, -120.59228365935401, 83.14231129485714, -29.79904335273614)


def cosine_turns(u):
    whole = (u + magic) - magic
    frac = u - whole
    square = frac * frac
    acc = jnp.full_like(square, COS[-1])
    for coef in COS[-2::-1]:
        acc = acc * square + coef
    return acc


def feature_kernel(emb_ref, freq_ref, base_ref, full_ref, treated_ref, counter_ref, feat_ref, moment_ref):
    @pl.when(pl.program_id(0) == 0)
    def _():
        moment_ref[...] = jnp.zeros_like(moment_ref)

    scaled = jnp.dot(emb_ref[...], freq_ref[...], preferred_element_type=jnp.float32) * turn
    base, full = base_ref[...], full_ref[...]
    observed = cosine_turns(scaled + jnp.where(treated_ref[...] > 0.5, full, base))
    counterfactual = cosine_turns(scaled + jnp.where(counter_ref[...] > 0.5, full, base))
    feat_ref[...] = observed.astype(jnp.bfloat16)
    moment_ref[...] += jnp.sum(counterfactual - observed, axis=0, keepdims=True)


def make_features(emb, freq, base, full, treated, counter):
    count, emb_width = emb.shape
    width = freq.shape[1]
    step = 256
    whole = lambda shape: pl.BlockSpec(shape, lambda i: (0, 0))
    return pl.pallas_call(
        feature_kernel,
        grid=(count // step,),
        in_specs=[
            pl.BlockSpec((step, emb_width), lambda i: (i, 0)),
            whole((emb_width, width)),
            whole((1, width)),
            whole((1, width)),
            pl.BlockSpec((step, 1), lambda i: (i, 0)),
            pl.BlockSpec((step, 1), lambda i: (i, 0)),
        ],
        out_specs=[pl.BlockSpec((step, width), lambda i: (i, 0)), whole((1, width))],
        out_shape=[
            jax.ShapeDtypeStruct((count, width), jnp.bfloat16),
            jax.ShapeDtypeStruct((1, width), jnp.float32),
        ],
        cost_estimate=pl.CostEstimate(
            flops=2 * count * emb_width * width, bytes_accessed=2 * count * emb_width, transcendentals=2 * count * width
        ),
        compiler_params=pltpu.CompilerParams(vmem_limit_bytes=VMEM_BYTES),
    )(emb, freq, base, full, treated, counter)


def inverse_factor(tile):
    groups = TILE // 8
    sub = lax.broadcasted_iota(jnp.int32, (8, TILE), 0)
    lane = lax.broadcasted_iota(jnp.int32, (8, TILE), 1)
    left = [tile[8 * g : 8 * g + 8, :] for g in range(groups)]
    right = [jnp.where(lane == sub + 8 * g, 1.0, 0.0) for g in range(groups)]
    for j in range(TILE):
        g, t = divmod(j, 8)
        row = left[g][t : t + 1, :]
        scale = 1.0 / row[:, j : j + 1]
        left_row = row * scale
        right_row = right[g][t : t + 1, :] * scale
        for i in range(g, groups):
            col = left[i][:, j : j + 1]
            if i == g:
                col = jnp.where(sub[:, :1] > t, col, 0.0)
            left[i] = left[i] - col * left_row
            right[i] = right[i] - col * right_row
    out = []
    for g in range(groups):
        diag = jnp.sum(jnp.where(lane == sub + 8 * g, left[g], 0.0), axis=1, keepdims=True)
        out.append(right[g] * (1.0 / jnp.sqrt(diag)))
    return jnp.concatenate(out, axis=0)


def split(value):
    high = value.astype(jnp.bfloat16)
    return high, (value - high.astype(jnp.float32)).astype(jnp.bfloat16)


def solve_kernel(
    sample_count,
    shift_ref,
    pivot_ref,
    cross_ref,
    moment_ref,
    moment_panel_ref,
    inv_high_ref,
    inv_low_ref,
    cross_high_ref,
    cross_low_ref,
    reduced_ref,
    x_ref,
):
    width = cross_ref.shape[1]
    start = 2 * PANEL
    rows = lax.broadcasted_iota(jnp.int32, (PANEL, PANEL), 0)
    cols = lax.broadcasted_iota(jnp.int32, (PANEL, PANEL), 1)
    eye = jnp.where(rows == cols, 1.0, 0.0)
    x_ref[:, 0:PANEL] = pivot_ref[...] / sample_count + ridge * eye
    x_ref[:, PANEL:start] = eye
    rows = lax.broadcasted_iota(jnp.int32, (PANEL, width), 0)
    cols = lax.broadcasted_iota(jnp.int32, (PANEL, width), 1)
    own = jnp.where(rows == cols + shift_ref[0], ridge, 0.0)
    x_ref[:, start : start + width] = cross_ref[...] / sample_count + own
    column = jnp.sum(eye * (moment_panel_ref[...] / sample_count), axis=1, keepdims=True)
    x_ref[:, start + width :] = jnp.broadcast_to(column, (PANEL, LANES))

    def block(b, carry):
        at = pl.multiple_of(b * TILE, TILE)
        inverse = inverse_factor(x_ref[pl.ds(at, TILE), pl.ds(at, TILE)])
        solved = jnp.dot(inverse, x_ref[pl.ds(at, TILE), :], precision=lax.Precision.HIGHEST, preferred_element_type=jnp.float32)
        lanes = lax.broadcasted_iota(jnp.int32, (TILE, PANEL), 1)
        coef = jnp.where(lanes >= at + TILE, solved[:, :PANEL], 0.0)
        x_ref[...] -= jnp.dot(coef.T, solved, precision=lax.Precision.HIGHEST, preferred_element_type=jnp.float32)
        x_ref[pl.ds(at, TILE), :] = solved
        return carry

    lax.fori_loop(0, PANEL // TILE, block, 0)
    inv_high_ref[...], inv_low_ref[...] = split(x_ref[:, PANEL:start].T)
    cross = x_ref[:, start : start + width]
    cross_high_ref[...], cross_low_ref[...] = split(cross)
    solved = x_ref[:, start + width : start + width + 1]
    reduced = moment_ref[...] / sample_count - jnp.sum(cross * solved, axis=0, keepdims=True)
    reduced_ref[...] = jnp.sqrt(jnp.float32(sample_count)) * reduced


def eliminate(sample_count, shift, pivot, cross, moment, moment_panel):
    width = cross.shape[1]
    vmem = pl.BlockSpec(memory_space=pltpu.VMEM)
    square = jax.ShapeDtypeStruct((PANEL, PANEL), jnp.bfloat16)
    wide = jax.ShapeDtypeStruct((PANEL, width), jnp.bfloat16)
    return pl.pallas_call(
        functools.partial(solve_kernel, sample_count),
        in_specs=[pl.BlockSpec(memory_space=pltpu.SMEM)] + [vmem] * 4,
        out_specs=[vmem] * 5,
        out_shape=[square, square, wide, wide, jax.ShapeDtypeStruct((1, width), jnp.float32)],
        scratch_shapes=[pltpu.VMEM((PANEL, 2 * PANEL + width + LANES), jnp.float32)],
        cost_estimate=pl.CostEstimate(flops=40 * 10**9, bytes_accessed=4 * 10**6, transcendentals=0),
        compiler_params=pltpu.CompilerParams(vmem_limit_bytes=VMEM_BYTES),
    )(shift, pivot, cross, moment, moment_panel)


def three_pass(left, right_high, right_low):
    high, low = split(left)
    dot = functools.partial(jnp.dot, preferred_element_type=jnp.float32)
    return dot(high, right_high) + (dot(high, right_low) + dot(low, right_high))


def main_kernel(
    sample_count,
    order_ref,
    place_ref,
    freq_ref,
    base_ref,
    full_ref,
    emb_ref,
    treated_ref,
    feat_ref,
    feat_panel_ref,
    inv_high_ref,
    inv_low_ref,
    cross_high_ref,
    cross_low_ref,
    schur_ref,
    panel_ref,
):
    height = freq_ref.shape[0]
    count = emb_ref.shape[1]
    width = feat_ref.shape[1]
    base, full = base_ref[...], full_ref[...]
    own = jnp.zeros((height, width), jnp.float32)
    panel = jnp.zeros((height, PANEL), jnp.float32)
    step = 512
    for at in range(0, count, step):
        scaled = jnp.dot(freq_ref[...], emb_ref[:, at : at + step], preferred_element_type=jnp.float32) * turn
        phase = jnp.where(treated_ref[:, at : at + step] > 0.5, full, base)
        features = cosine_turns(scaled + phase).astype(jnp.bfloat16)
        own += jnp.dot(features, feat_ref[at : at + step, :], preferred_element_type=jnp.float32)
        panel += jnp.dot(features, feat_panel_ref[at : at + step, :], preferred_element_type=jnp.float32)
    first = place_ref[0] + order_ref[pl.program_id(0)] * height
    rows = first + lax.broadcasted_iota(jnp.int32, (height, width), 0)
    cols = place_ref[1] + lax.broadcasted_iota(jnp.int32, (height, width), 1)
    own = own / sample_count + jnp.where(rows == cols, ridge, 0.0)
    rows = first + lax.broadcasted_iota(jnp.int32, (height, PANEL), 0)
    cols = place_ref[2] + lax.broadcasted_iota(jnp.int32, (height, PANEL), 1)
    panel = panel / sample_count + jnp.where(rows == cols, ridge, 0.0)
    factor = three_pass(panel, inv_high_ref[...], inv_low_ref[...])
    panel_ref[...] = factor
    schur_ref[...] = own - three_pass(factor, cross_high_ref[...], cross_low_ref[...])


def main(order, place, freqs, base, full, emb_t, treated, feat, feat_panel, solved):
    blocks = order.shape[0]
    row_height, emb_width = freqs.shape
    height = row_height // blocks
    count, width = feat.shape
    fixed = lambda array: pl.BlockSpec(array.shape, lambda i, order, place: (0, 0), pipeline_mode=pl.Buffered(1))
    moved = lambda cols: pl.BlockSpec((height, cols), lambda i, order, place: (order[i], 0))
    flops = 2 * row_height * (count * (emb_width + width + PANEL) + 3 * PANEL * (PANEL + width))
    return pl.pallas_call(
        functools.partial(main_kernel, count),
        grid_spec=pltpu.PrefetchScalarGridSpec(
            num_scalar_prefetch=2,
            grid=(blocks,),
            in_specs=[
                pl.BlockSpec((height, emb_width), lambda i, order, place: (i, 0)),
                moved(1),
                moved(1),
                fixed(emb_t),
                fixed(treated),
                fixed(feat),
                fixed(feat_panel),
            ]
            + [fixed(array) for array in solved],
            out_specs=[moved(width), moved(PANEL)],
        ),
        out_shape=[
            jax.ShapeDtypeStruct((row_height, width), jnp.float32),
            jax.ShapeDtypeStruct((row_height, PANEL), jnp.float32),
        ],
        cost_estimate=pl.CostEstimate(flops=flops, bytes_accessed=30 * 10**6, transcendentals=count * row_height),
        compiler_params=pltpu.CompilerParams(vmem_limit_bytes=VMEM_BYTES),
    )(order, place, freqs, base, full, emb_t, treated, feat, feat_panel, *solved)


def gather_rows_staged(freq_t, samp_index, feat_index):
    half = 8
    mates = [(s * 16 + f, s * 16 + (f ^ half)) for s in range(2) for f in range(s * half, (s + 1) * half)]

    def swap(value, bits):
        return lax.ppermute(value, "feat", [(f, f ^ bits) for f in range(16)])

    crossed = lax.ppermute(freq_t, ("samp", "feat"), mates)
    mine = jnp.where(feat_index // half == samp_index, freq_t, crossed)
    near = [mine, swap(mine, 4), swap(mine, 2), swap(mine, 6)]
    other = [swap(block, 1) for block in near]
    order = jnp.bitwise_xor(feat_index % half, jnp.array([0, 4, 2, 6, 1, 5, 3, 7], jnp.int32))
    return jnp.concatenate(near + other, axis=0), order


def gather_samples_staged(embeddings, marks, samp_index, feat_index):
    part = embeddings.shape[0] // 2
    core = feat_index % 2
    mine = lax.dynamic_slice_in_dim(embeddings, core * part, part, 0)
    got = lax.ppermute(mine, "samp", [(0, 1), (1, 0)])
    got_mate = lax.ppermute(got, "feat", [(f, f ^ 1) for f in range(16)])
    lower = jnp.where(core == 0, got, got_mate)
    upper = jnp.where(core == 0, got_mate, got)
    other = jnp.concatenate([lower, upper], axis=0)
    first = samp_index == 0
    emb = jnp.concatenate([jnp.where(first, embeddings, other), jnp.where(first, other, embeddings)], axis=0)
    other_marks = lax.ppermute(marks, "samp", [(0, 1), (1, 0)])
    marks = jnp.concatenate(
        [jnp.where(first, marks, other_marks), jnp.where(first, other_marks, marks)], axis=1
    )
    return emb, marks


def per_device(embeddings, frequencies, phases, treat_freq, treatment, flips, panel):
    samp_size = lax.axis_size("samp")
    feat_size = lax.axis_size("feat")
    samp_index = lax.axis_index("samp")
    feat_index = lax.axis_index("feat")
    emb_width, col_width = frequencies.shape
    feat_total = col_width * feat_size
    row_height = feat_total // samp_size
    first_col = panel[0] * PANEL
    first_dev = first_col // col_width
    staged = samp_size == 2 and feat_size == 16

    panel_freq = []
    for member in range(PANEL // col_width):
        own = feat_index == first_dev + member
        panel_freq.append(lax.psum(jnp.where(own, frequencies, jnp.zeros_like(frequencies)), "feat"))
    panel_freq = jnp.concatenate(panel_freq, axis=1)

    treated = treatment.astype(jnp.float32)
    flipped = flips.astype(jnp.float32)
    counter = treated + flipped - 2.0 * treated * flipped
    marks = jnp.stack([treated, counter])
    base_own = phases * turn
    turns = lax.all_gather(jnp.stack([base_own, base_own + treat_freq * turn]), "feat", axis=1, tiled=True)
    if staged:
        emb, marks = gather_samples_staged(embeddings, marks, samp_index, feat_index)
        freqs, order = gather_rows_staged(frequencies.T, samp_index, feat_index)
    else:
        emb = lax.all_gather(embeddings, "samp", axis=0, tiled=True)
        marks = lax.all_gather(marks, "samp", axis=1, tiled=True)
        freqs = lax.all_gather(frequencies.T, "feat", axis=0, tiled=True)
        freqs = lax.dynamic_slice_in_dim(freqs, samp_index * row_height, row_height, 0)
        order = jnp.arange(row_height // col_width, dtype=jnp.int32)
    treated_col, counter_col = marks[0][:, None], marks[1][:, None]
    count = emb.shape[0]

    own_turns = lax.dynamic_slice_in_dim(turns, feat_index * col_width, col_width, 1)
    panel_turns = lax.dynamic_slice_in_dim(turns, first_col, PANEL, 1)
    row_turns = lax.dynamic_slice_in_dim(turns, samp_index * row_height, row_height, 1)
    feat, moment = make_features(emb, frequencies, own_turns[:1], own_turns[1:], treated_col, counter_col)
    feat_panel, moment_panel = make_features(
        emb, panel_freq, panel_turns[:1], panel_turns[1:], treated_col, counter_col
    )
    inner = lambda left, right: lax.dot_general(
        left, right, (((0,), (0,)), ((), ())), preferred_element_type=jnp.float32
    )
    pivot = inner(feat_panel, feat_panel)
    cross = inner(feat_panel, feat)
    own_col = feat_index * col_width
    shift = (own_col - first_col).reshape(1).astype(jnp.int32)
    *solved, reduced = eliminate(count, shift, pivot, cross, moment, moment_panel)
    place = jnp.stack([samp_index * row_height, own_col, first_col]).astype(jnp.int32)
    schur, panel_factor = main(
        order,
        place,
        freqs,
        row_turns[0][:, None],
        row_turns[1][:, None],
        emb.T,
        marks[:1],
        feat,
        feat_panel,
        solved,
    )
    return schur, panel_factor, reduced[0]


def solution(mesh):
    return jax.shard_map(
        per_device,
        mesh=mesh,
        in_specs=(
            P("samp", None),
            P(None, "feat"),
            P("feat"),
            P("feat"),
            P("samp"),
            P("samp"),
            P(),
        ),
        out_specs=(P("samp", "feat"), P("samp", None), P("feat")),
        check_vma=False,
    )
```

```python
import functools

import jax
import jax.numpy as jnp
from jax import lax
from jax.experimental import pallas as pl
from jax.experimental.pallas import tpu as pltpu
from jax.sharding import PartitionSpec as P

PANEL = 512
TILE = 128
LANES = 128

ridge = 0.1
turn = 0.15915494309189535
magic = 12582912.0
VMEM_BYTES = 58 * 1024 * 1024
COS = (1.4142124462507522, -27.915133726537626, 91.8229879115028, -120.59228365935401, 83.14231129485714, -29.79904335273614)


def cosine_turns(u):
    whole = (u + magic) - magic
    frac = u - whole
    square = frac * frac
    acc = jnp.full_like(square, COS[-1])
    for coef in COS[-2::-1]:
        acc = acc * square + coef
    return acc


def split(value):
    high = value.astype(jnp.bfloat16)
    return high, (value - high.astype(jnp.float32)).astype(jnp.bfloat16)


def thirds(value):
    high = lax.reduce_precision(value, 8, 7)
    middle = lax.reduce_precision(value - high, 8, 7)
    low = value - high - middle
    return [part.astype(jnp.bfloat16) for part in (high, middle, low)]


def feature_kernel(pos_ref, emb_ref, freq_ref, treated_ref, counter_ref, feat_ref, moment_ref):
    @pl.when(pl.program_id(0) == 0)
    def _():
        moment_ref[...] = jnp.zeros_like(moment_ref)

    width = emb_ref.shape[1]
    parts = [freq_ref[width + k : width + k + 1, :].astype(jnp.float32) for k in range(6)]
    base = (parts[0] + parts[1]) + parts[2]
    full = (parts[3] + parts[4]) + parts[5]
    scaled = jnp.dot(emb_ref[...], freq_ref[:width, :], preferred_element_type=jnp.float32) * turn
    observed = cosine_turns(scaled + jnp.where(treated_ref[...] > 0.5, full, base))
    counterfactual = cosine_turns(scaled + jnp.where(counter_ref[...] > 0.5, full, base))
    feat_ref[...] = observed.astype(jnp.bfloat16)
    moment_ref[...] += jnp.sum(counterfactual - observed, axis=0, keepdims=True)


def make_features(pos, emb, freq, treated, counter):
    count, emb_width = emb.shape
    rows, width = freq.shape
    step = 256
    ratio = count // pos.shape[0] // step
    whole = lambda shape: pl.BlockSpec(shape, lambda i, pos: (0, 0))
    return pl.pallas_call(
        feature_kernel,
        grid_spec=pltpu.PrefetchScalarGridSpec(
            num_scalar_prefetch=1,
            grid=(count // step,),
            in_specs=[
                pl.BlockSpec((step, emb_width), lambda i, pos: (pos[i // ratio] * ratio + i % ratio, 0)),
                whole((rows, width)),
                pl.BlockSpec((step, 1), lambda i, pos: (i, 0)),
                pl.BlockSpec((step, 1), lambda i, pos: (i, 0)),
            ],
            out_specs=[pl.BlockSpec((step, width), lambda i, pos: (i, 0)), whole((1, width))],
        ),
        out_shape=[
            jax.ShapeDtypeStruct((count, width), jnp.bfloat16),
            jax.ShapeDtypeStruct((1, width), jnp.float32),
        ],
        cost_estimate=pl.CostEstimate(
            flops=2 * count * emb_width * width, bytes_accessed=2 * count * emb_width, transcendentals=2 * count * width
        ),
        compiler_params=pltpu.CompilerParams(vmem_limit_bytes=VMEM_BYTES),
    )(pos, emb, freq, treated, counter)


def inverse_factor(tile):
    groups = TILE // 8
    at_once = 4
    sub = lax.broadcasted_iota(jnp.int32, (8, TILE), 0)
    lane = lax.broadcasted_iota(jnp.int32, (8, TILE), 1)
    left = [tile[8 * g : 8 * g + 8, :] for g in range(groups)]
    right = [jnp.where(lane == sub + 8 * g, 1.0, 0.0) for g in range(groups)]
    spread = lambda value: jnp.broadcast_to(value, (8, TILE))
    for j in range(0, TILE, at_once):
        g, t = divmod(j, 8)
        ks = range(at_once)
        rows = [spread(left[g][t + k : t + k + 1, :]) for k in ks]
        marks = [spread(right[g][t + k : t + k + 1, :]) for k in ks]
        p = {(k, m): spread(rows[k][:, j + m : j + m + 1]) for k in ks for m in range(k, at_once)}
        f, inv = {}, []
        for k in ks:
            inv.append(1.0 / p[k, k])
            for m in range(k + 1, at_once):
                f[m, k] = p[k, m] * inv[k]
            for m in range(k + 1, at_once):
                for n in range(m, at_once):
                    p[m, n] = p[m, n] - f[m, k] * p[k, n]
        for k in ks:
            for q in range(k):
                rows[k] = rows[k] - f[k, q] * rows[q]
                marks[k] = marks[k] - f[k, q] * marks[q]
        row_part, mark_part = [None] * at_once, [None] * at_once
        for k in reversed(ks):
            row_part[k] = rows[k] * inv[k]
            mark_part[k] = marks[k] * inv[k]
            for q in range(k + 1, at_once):
                row_part[k] = row_part[k] - f[q, k] * row_part[q]
                mark_part[k] = mark_part[k] - f[q, k] * mark_part[q]
        for i in range(g, groups):
            if i > g or t + at_once < 8:
                cols = [spread(left[i][:, j + k : j + k + 1]) for k in ks]
                if i == g:
                    cols = [jnp.where(sub >= t + at_once, col, 0.0) for col in cols]
                left_sum = (cols[0] * row_part[0] + cols[1] * row_part[1]) + (cols[2] * row_part[2] + cols[3] * row_part[3])
                right_sum = (cols[0] * mark_part[0] + cols[1] * mark_part[1]) + (cols[2] * mark_part[2] + cols[3] * mark_part[3])
                left[i] = left[i] - left_sum
                right[i] = right[i] - right_sum
        for k in ks:
            left[g] = jnp.where(sub == t + k, rows[k], left[g])
            right[g] = jnp.where(sub == t + k, marks[k], right[g])
    out = []
    for g in range(groups):
        diag = jnp.sum(jnp.where(lane == sub + 8 * g, left[g], 0.0), axis=1, keepdims=True)
        out.append(right[g] * (1.0 / jnp.sqrt(diag)))
    return jnp.concatenate(out, axis=0)


def eliminate_blocks(x_ref, first, last):
    def block(b, carry):
        at = pl.multiple_of(b * TILE, TILE)
        inverse = inverse_factor(x_ref[pl.ds(at, TILE), pl.ds(at, TILE)])
        solved = jnp.dot(inverse, x_ref[pl.ds(at, TILE), :], precision=lax.Precision.HIGHEST, preferred_element_type=jnp.float32)
        lanes = lax.broadcasted_iota(jnp.int32, (TILE, PANEL), 1)

        @pl.when(b < PANEL // TILE - 1)
        def _():
            coef = jnp.where(lanes >= at + TILE, solved[:, :PANEL], 0.0)
            x_ref[...] -= jnp.dot(coef.T, solved, precision=lax.Precision.HIGHEST, preferred_element_type=jnp.float32)

        x_ref[pl.ds(at, TILE), :] = solved
        return carry

    lax.fori_loop(first, last, block, 0)


def front_kernel(sample_count, shift_ref, feat_panel_ref, feat_ref, moment_panel_ref, x_ref):
    width = feat_ref.shape[1]
    start = 2 * PANEL
    panel_t = feat_panel_ref[...].T
    dot = functools.partial(jnp.dot, preferred_element_type=jnp.float32)
    rows = lax.broadcasted_iota(jnp.int32, (PANEL, PANEL), 0)
    cols = lax.broadcasted_iota(jnp.int32, (PANEL, PANEL), 1)
    eye = jnp.where(rows == cols, 1.0, 0.0)
    x_ref[:, 0:PANEL] = dot(panel_t, feat_panel_ref[...]) / sample_count + ridge * eye
    x_ref[:, PANEL:start] = eye
    rows = lax.broadcasted_iota(jnp.int32, (PANEL, width), 0)
    cols = lax.broadcasted_iota(jnp.int32, (PANEL, width), 1)
    own = jnp.where(rows == cols + shift_ref[0], ridge, 0.0)
    x_ref[:, start : start + width] = dot(panel_t, feat_ref[...]) / sample_count + own
    column = jnp.sum(eye * (moment_panel_ref[...] / sample_count), axis=1, keepdims=True)
    x_ref[:, start + width :] = jnp.broadcast_to(column, (PANEL, LANES))
    eliminate_blocks(x_ref, 0, PANEL // TILE // 2)


def back_kernel(sample_count, x_in_ref, moment_ref, inv_high_ref, inv_low_ref, cross_high_ref, cross_low_ref, reduced_ref, x_ref):
    width = moment_ref.shape[1]
    start = 2 * PANEL
    x_ref[...] = x_in_ref[...]
    eliminate_blocks(x_ref, PANEL // TILE // 2, PANEL // TILE)
    inv_high_ref[...], inv_low_ref[...] = split(x_ref[:, PANEL:start].T)
    cross = x_ref[:, start : start + width]
    cross_high_ref[...], cross_low_ref[...] = split(cross)
    solved = x_ref[:, start + width : start + width + 1]
    reduced = moment_ref[...] / sample_count - jnp.sum(cross * solved, axis=0, keepdims=True)
    reduced_ref[...] = jnp.sqrt(jnp.float32(sample_count)) * reduced


def eliminate_front(shift, feat_panel, feat, moment_panel):
    count, width = feat.shape
    vmem = pl.BlockSpec(memory_space=pltpu.VMEM)
    return pl.pallas_call(
        functools.partial(front_kernel, count),
        in_specs=[pl.BlockSpec(memory_space=pltpu.SMEM)] + [vmem] * 3,
        out_specs=vmem,
        out_shape=jax.ShapeDtypeStruct((PANEL, 2 * PANEL + width + LANES), jnp.float32),
        cost_estimate=pl.CostEstimate(flops=20 * 10**9, bytes_accessed=8 * 10**6, transcendentals=0),
        compiler_params=pltpu.CompilerParams(vmem_limit_bytes=VMEM_BYTES),
    )(shift, feat_panel, feat, moment_panel)


def eliminate_back(count, state, moment):
    width = moment.shape[1]
    vmem = pl.BlockSpec(memory_space=pltpu.VMEM)
    square = jax.ShapeDtypeStruct((PANEL, PANEL), jnp.bfloat16)
    wide = jax.ShapeDtypeStruct((PANEL, width), jnp.bfloat16)
    return pl.pallas_call(
        functools.partial(back_kernel, count),
        in_specs=[vmem] * 2,
        out_specs=[vmem] * 5,
        out_shape=[square, square, wide, wide, jax.ShapeDtypeStruct((1, width), jnp.float32)],
        scratch_shapes=[pltpu.VMEM(state.shape, jnp.float32)],
        cost_estimate=pl.CostEstimate(flops=20 * 10**9, bytes_accessed=8 * 10**6, transcendentals=0),
        compiler_params=pltpu.CompilerParams(vmem_limit_bytes=VMEM_BYTES),
    )(state, moment)


def three_pass(left, right_high, right_low):
    high, low = split(left)
    dot = functools.partial(jnp.dot, preferred_element_type=jnp.float32)
    return dot(high, right_high) + (dot(high, right_low) + dot(low, right_high))


def main_kernel(
    sample_count,
    blocks,
    order_ref,
    place_ref,
    pos_ref,
    *refs,
):
    freq_refs = refs[:blocks]
    (
        emb_ref,
        treated_ref,
        feat_ref,
        feat_panel_ref,
        inv_high_ref,
        inv_low_ref,
        cross_high_ref,
        cross_low_ref,
        schur_ref,
        panel_ref,
        slots,
        sems,
    ) = refs[blocks:]
    now = pl.program_id(0)

    def fetch(index, slot):
        for k in range(blocks):

            @pl.when(index == k)
            def _():
                pltpu.make_async_copy(freq_refs[k], slots.at[slot], sems.at[slot]).start()

    @pl.when(now == 0)
    def _():
        fetch(0, 0)

    fetch(now + 1, lax.rem(now + 1, 2))
    slot = lax.rem(now, 2)
    pltpu.make_async_copy(freq_refs[0], slots.at[slot], sems.at[slot]).wait()

    height = slots.shape[1]
    count, emb_width = emb_ref.shape
    width = feat_ref.shape[1]
    parts = slots[slot, :, emb_width : emb_width + LANES].astype(jnp.float32)
    base = (parts[:, 0:1] + parts[:, 1:2]) + parts[:, 2:3]
    full = (parts[:, 3:4] + parts[:, 4:5]) + parts[:, 5:6]
    own = jnp.zeros((height, width), jnp.float32)
    panel = jnp.zeros((height, PANEL), jnp.float32)
    step = count // pos_ref.shape[0]
    for j in range(count // step):
        at = j * step
        emb = emb_ref[pl.ds(pl.multiple_of(pos_ref[j] * step, step), step), :]
        scaled = lax.dot_general(
            slots[slot, :, :emb_width], emb, (((1,), (1,)), ((), ())), preferred_element_type=jnp.float32
        )
        phase = jnp.where(treated_ref[:, at : at + step] > 0.5, full, base)
        features = cosine_turns(scaled * turn + phase).astype(jnp.bfloat16)
        own += jnp.dot(features, feat_ref[at : at + step, :], preferred_element_type=jnp.float32)
        panel += jnp.dot(features, feat_panel_ref[at : at + step, :], preferred_element_type=jnp.float32)
    first = place_ref[0] + order_ref[now] * height
    rows = first + lax.broadcasted_iota(jnp.int32, (height, width), 0)
    cols = place_ref[1] + lax.broadcasted_iota(jnp.int32, (height, width), 1)
    own = own / sample_count + jnp.where(rows == cols, ridge, 0.0)
    rows = first + lax.broadcasted_iota(jnp.int32, (height, PANEL), 0)
    cols = place_ref[2] + lax.broadcasted_iota(jnp.int32, (height, PANEL), 1)
    panel = panel / sample_count + jnp.where(rows == cols, ridge, 0.0)
    factor = three_pass(panel, inv_high_ref[...], inv_low_ref[...])
    panel_ref[...] = factor
    schur_ref[...] = own - three_pass(factor, cross_high_ref[...], cross_low_ref[...])


def main(order, place, pos, freqs, emb, treated, feat, feat_panel, solved):
    blocks = len(freqs)
    height = freqs[0].shape[0]
    row_height = blocks * height
    emb_width = emb.shape[1]
    count, width = feat.shape
    fixed = lambda array: pl.BlockSpec(array.shape, lambda i, *_: (0, 0), pipeline_mode=pl.Buffered(1))
    moved = lambda cols: pl.BlockSpec((height, cols), lambda i, order, *_: (order[i], 0))
    flops = 2 * row_height * (count * (emb_width + width + PANEL) + 3 * PANEL * (PANEL + width))
    return pl.pallas_call(
        functools.partial(main_kernel, count, blocks),
        grid_spec=pltpu.PrefetchScalarGridSpec(
            num_scalar_prefetch=3,
            grid=(blocks,),
            in_specs=[pl.BlockSpec(memory_space=pl.ANY)] * blocks
            + [fixed(array) for array in (emb, treated, feat, feat_panel, *solved)],
            out_specs=[moved(width), moved(PANEL)],
            scratch_shapes=[
                pltpu.VMEM((2, height, freqs[0].shape[1]), jnp.bfloat16),
                pltpu.SemaphoreType.DMA((2,)),
            ],
        ),
        out_shape=[
            jax.ShapeDtypeStruct((row_height, width), jnp.float32),
            jax.ShapeDtypeStruct((row_height, PANEL), jnp.float32),
        ],
        cost_estimate=pl.CostEstimate(flops=flops, bytes_accessed=30 * 10**6, transcendentals=count * row_height),
        compiler_params=pltpu.CompilerParams(vmem_limit_bytes=VMEM_BYTES),
    )(order, place, pos, *freqs, emb, treated, feat, feat_panel, *solved)


def swap(value, bits):
    return lax.ppermute(value, "feat", [(f, f ^ bits) for f in range(lax.axis_size("feat"))])


def gather_samples_staged(embeddings, marks, samp_index, feat_index):
    part = embeddings.shape[0] // 2
    core = feat_index % 2
    mine = lax.dynamic_slice_in_dim(embeddings, core * part, part, 0)
    got = lax.ppermute(mine, "samp", [(0, 1), (1, 0)])
    other_marks = lax.ppermute(marks, "samp", [(0, 1), (1, 0)])
    emb = jnp.concatenate([embeddings, got, swap(got, 1)], axis=0)
    piece = jnp.arange(4, dtype=jnp.int32)
    pos = jnp.where(piece // 2 == samp_index, piece % 2, jnp.where(piece % 2 == core, 2, 3))
    first = samp_index == 0
    marks = jnp.concatenate([jnp.where(first, marks, other_marks), jnp.where(first, other_marks, marks)], axis=1)
    return emb, marks, pos.astype(jnp.int32)


def per_device(embeddings, frequencies, phases, treat_freq, treatment, flips, panel):
    samp_size = lax.axis_size("samp")
    feat_size = lax.axis_size("feat")
    samp_index = lax.axis_index("samp")
    feat_index = lax.axis_index("feat")
    emb_width, col_width = frequencies.shape
    feat_total = col_width * feat_size
    row_height = feat_total // samp_size
    first_col = panel[0] * PANEL
    first_dev = first_col // col_width
    staged = samp_size == 2 and feat_size == 16
    half = 8

    base = phases * turn
    parts = jnp.stack(thirds(base) + thirds(base + treat_freq * turn))
    freq = jnp.concatenate([frequencies, jnp.pad(parts, ((0, 10), (0, 0)))], axis=0)
    freq_t = jnp.concatenate([frequencies.T, jnp.pad(parts.T, ((0, 0), (0, LANES - 6)))], axis=1)

    treated = treatment.astype(jnp.float32)
    flipped = flips.astype(jnp.float32)
    counter = treated + flipped - 2.0 * treated * flipped
    marks = jnp.stack([treated, counter])
    if staged:
        emb, marks, pos = gather_samples_staged(embeddings, marks, samp_index, feat_index)
        mates = [(s * 16 + f, s * 16 + (f ^ half)) for s in range(2) for f in range(s * half, (s + 1) * half)]
        crossed = lax.ppermute(freq_t, ("samp", "feat"), mates)
        mine = jnp.where(feat_index // half == samp_index, freq_t, crossed)
    else:
        emb = lax.all_gather(embeddings, "samp", axis=0, tiled=True)
        marks = lax.all_gather(marks, "samp", axis=1, tiled=True)
        pos = jnp.arange(emb.shape[0] // 512, dtype=jnp.int32)

    panel_freq = []
    for member in range(PANEL // col_width):
        own = feat_index == first_dev + member
        panel_freq.append(lax.psum(jnp.where(own, freq, jnp.zeros_like(freq)), "feat"))
    panel_freq = jnp.concatenate(panel_freq, axis=1)

    treated_col, counter_col = marks[0][:, None], marks[1][:, None]
    feat, moment = make_features(pos, emb, freq, treated_col, counter_col)
    if staged:
        mine, panel_freq, feat = lax.optimization_barrier((mine, panel_freq, feat))
        near = [swap(mine, 4), swap(mine, 2), swap(mine, 6)]
    feat_panel, moment_panel = make_features(pos, emb, panel_freq, treated_col, counter_col)
    own_col = feat_index * col_width
    shift = (own_col - first_col).reshape(1).astype(jnp.int32)
    state = eliminate_front(shift, feat_panel, feat, moment_panel)
    if staged:
        state, near = lax.optimization_barrier((state, near))
        near = [mine] + near
        freqs = near + [swap(block, 1) for block in near]
        order = jnp.bitwise_xor(feat_index % half, jnp.array([0, 4, 2, 6, 1, 5, 3, 7], jnp.int32))
    else:
        rows = lax.all_gather(freq_t, "feat", axis=0, tiled=True)
        rows = lax.dynamic_slice_in_dim(rows, samp_index * row_height, row_height, 0)
        freqs = jnp.split(rows, row_height // col_width, axis=0)
        order = jnp.arange(row_height // col_width, dtype=jnp.int32)
    *solved, reduced = eliminate_back(emb.shape[0], state, moment)
    place = jnp.stack([samp_index * row_height, own_col, first_col]).astype(jnp.int32)
    schur, panel_factor = main(order, place, pos, freqs, emb, marks[:1], feat, feat_panel, solved)
    return schur, panel_factor, reduced[0]


def solution(mesh):
    return jax.shard_map(
        per_device,
        mesh=mesh,
        in_specs=(
            P("samp", None),
            P(None, "feat"),
            P("feat"),
            P("feat"),
            P("samp"),
            P("samp"),
            P(),
        ),
        out_specs=(P("samp", "feat"), P("samp", None), P("feat")),
        check_vma=False,
    )
```

```python
import functools

import jax
import jax.numpy as jnp
from jax import lax
from jax.experimental import pallas as pl
from jax.experimental.pallas import tpu as pltpu
from jax.sharding import PartitionSpec as P

PANEL = 512
TILE = 128
LANES = 128

ridge = 0.1
turn = 0.15915494309189535
magic = 12582912.0
VMEM_BYTES = 58 * 1024 * 1024
COS = (1.4142124462507522, -27.915133726537626, 91.8229879115028, -120.59228365935401, 83.14231129485714, -29.79904335273614)


def cosine_turns(u):
    whole = (u + magic) - magic
    frac = u - whole
    square = frac * frac
    acc = jnp.full_like(square, COS[-1])
    for coef in COS[-2::-1]:
        acc = acc * square + coef
    return acc


def split(value):
    high = value.astype(jnp.bfloat16)
    return high, (value - high.astype(jnp.float32)).astype(jnp.bfloat16)


def thirds(value):
    high = lax.reduce_precision(value, 8, 7)
    middle = lax.reduce_precision(value - high, 8, 7)
    low = value - high - middle
    return [part.astype(jnp.bfloat16) for part in (high, middle, low)]


def feature_kernel(pos_ref, emb_ref, freq_ref, treated_ref, counter_ref, feat_ref, moment_ref):
    @pl.when(pl.program_id(0) == 0)
    def _():
        moment_ref[...] = jnp.zeros_like(moment_ref)

    width = emb_ref.shape[1]
    parts = freq_ref[:, width:].astype(jnp.float32).T
    base = (parts[0:1] + parts[1:2]) + parts[2:3]
    full = (parts[3:4] + parts[4:5]) + parts[5:6]
    scaled = lax.dot_general(
        emb_ref[...], freq_ref[:, :width], (((1,), (1,)), ((), ())), preferred_element_type=jnp.float32
    ) * turn
    observed = cosine_turns(scaled + jnp.where(treated_ref[...] > 0.5, full, base))
    counterfactual = cosine_turns(scaled + jnp.where(counter_ref[...] > 0.5, full, base))
    feat_ref[...] = observed.astype(jnp.bfloat16)
    moment_ref[...] += jnp.sum(counterfactual - observed, axis=0, keepdims=True)


def make_features(pos, emb, freq, treated, counter):
    count, emb_width = emb.shape
    width = freq.shape[0]
    step = 256
    ratio = count // pos.shape[0] // step
    whole = lambda shape: pl.BlockSpec(shape, lambda i, pos: (0, 0))
    return pl.pallas_call(
        feature_kernel,
        grid_spec=pltpu.PrefetchScalarGridSpec(
            num_scalar_prefetch=1,
            grid=(count // step,),
            in_specs=[
                pl.BlockSpec((step, emb_width), lambda i, pos: (pos[i // ratio] * ratio + i % ratio, 0)),
                whole(freq.shape),
                pl.BlockSpec((step, 1), lambda i, pos: (i, 0)),
                pl.BlockSpec((step, 1), lambda i, pos: (i, 0)),
            ],
            out_specs=[pl.BlockSpec((step, width), lambda i, pos: (i, 0)), whole((1, width))],
        ),
        out_shape=[
            jax.ShapeDtypeStruct((count, width), jnp.bfloat16),
            jax.ShapeDtypeStruct((1, width), jnp.float32),
        ],
        cost_estimate=pl.CostEstimate(
            flops=2 * count * emb_width * width, bytes_accessed=2 * count * emb_width, transcendentals=2 * count * width
        ),
        compiler_params=pltpu.CompilerParams(vmem_limit_bytes=VMEM_BYTES),
    )(pos, emb, freq, treated, counter)


def inverse_factor(tile):
    groups = TILE // 8
    at_once = 4
    sub = lax.broadcasted_iota(jnp.int32, (8, TILE), 0)
    lane = lax.broadcasted_iota(jnp.int32, (8, TILE), 1)
    left = [tile[8 * g : 8 * g + 8, :] for g in range(groups)]
    right = [jnp.where(lane == sub + 8 * g, 1.0, 0.0) for g in range(groups)]
    spread = lambda value: jnp.broadcast_to(value, (8, TILE))
    for j in range(0, TILE, at_once):
        g, t = divmod(j, 8)
        ks = range(at_once)
        rows = [spread(left[g][t + k : t + k + 1, :]) for k in ks]
        marks = [spread(right[g][t + k : t + k + 1, :]) for k in ks]
        p = {(k, m): spread(rows[k][:, j + m : j + m + 1]) for k in ks for m in range(k, at_once)}
        f, inv = {}, []
        for k in ks:
            inv.append(1.0 / p[k, k])
            for m in range(k + 1, at_once):
                f[m, k] = p[k, m] * inv[k]
            for m in range(k + 1, at_once):
                for n in range(m, at_once):
                    p[m, n] = p[m, n] - f[m, k] * p[k, n]
        for k in ks:
            for q in range(k):
                rows[k] = rows[k] - f[k, q] * rows[q]
                marks[k] = marks[k] - f[k, q] * marks[q]
        row_part, mark_part = [None] * at_once, [None] * at_once
        for k in reversed(ks):
            row_part[k] = rows[k] * inv[k]
            mark_part[k] = marks[k] * inv[k]
            for q in range(k + 1, at_once):
                row_part[k] = row_part[k] - f[q, k] * row_part[q]
                mark_part[k] = mark_part[k] - f[q, k] * mark_part[q]
        for i in range(g, groups):
            if i > g or t + at_once < 8:
                cols = [spread(left[i][:, j + k : j + k + 1]) for k in ks]
                if i == g:
                    cols = [jnp.where(sub >= t + at_once, col, 0.0) for col in cols]
                left_sum = (cols[0] * row_part[0] + cols[1] * row_part[1]) + (cols[2] * row_part[2] + cols[3] * row_part[3])
                right_sum = (cols[0] * mark_part[0] + cols[1] * mark_part[1]) + (cols[2] * mark_part[2] + cols[3] * mark_part[3])
                left[i] = left[i] - left_sum
                right[i] = right[i] - right_sum
        for k in ks:
            left[g] = jnp.where(sub == t + k, rows[k], left[g])
            right[g] = jnp.where(sub == t + k, marks[k], right[g])
    out = []
    for g in range(groups):
        diag = jnp.sum(jnp.where(lane == sub + 8 * g, left[g], 0.0), axis=1, keepdims=True)
        out.append(right[g] * (1.0 / jnp.sqrt(diag)))
    return jnp.concatenate(out, axis=0)


def eliminate_blocks(x_ref, first, last):
    def block(b, carry):
        at = pl.multiple_of(b * TILE, TILE)
        inverse = inverse_factor(x_ref[pl.ds(at, TILE), pl.ds(at, TILE)])
        solved = jnp.dot(inverse, x_ref[pl.ds(at, TILE), :], precision=lax.Precision.HIGHEST, preferred_element_type=jnp.float32)
        lanes = lax.broadcasted_iota(jnp.int32, (TILE, PANEL), 1)

        @pl.when(b < PANEL // TILE - 1)
        def _():
            coef = jnp.where(lanes >= at + TILE, solved[:, :PANEL], 0.0)
            x_ref[...] -= jnp.dot(coef.T, solved, precision=lax.Precision.HIGHEST, preferred_element_type=jnp.float32)

        x_ref[pl.ds(at, TILE), :] = solved
        return carry

    lax.fori_loop(first, last, block, 0)


def front_kernel(sample_count, shift_ref, feat_panel_ref, feat_ref, moment_panel_ref, x_ref):
    width = feat_ref.shape[1]
    start = 2 * PANEL
    panel_t = feat_panel_ref[...].T
    dot = functools.partial(jnp.dot, preferred_element_type=jnp.float32)
    rows = lax.broadcasted_iota(jnp.int32, (PANEL, PANEL), 0)
    cols = lax.broadcasted_iota(jnp.int32, (PANEL, PANEL), 1)
    eye = jnp.where(rows == cols, 1.0, 0.0)
    x_ref[:, 0:PANEL] = dot(panel_t, feat_panel_ref[...]) / sample_count + ridge * eye
    x_ref[:, PANEL:start] = eye
    rows = lax.broadcasted_iota(jnp.int32, (PANEL, width), 0)
    cols = lax.broadcasted_iota(jnp.int32, (PANEL, width), 1)
    own = jnp.where(rows == cols + shift_ref[0], ridge, 0.0)
    x_ref[:, start : start + width] = dot(panel_t, feat_ref[...]) / sample_count + own
    column = jnp.sum(eye * (moment_panel_ref[...] / sample_count), axis=1, keepdims=True)
    x_ref[:, start + width :] = jnp.broadcast_to(column, (PANEL, LANES))
    eliminate_blocks(x_ref, 0, PANEL // TILE // 2)


def back_kernel(sample_count, x_in_ref, moment_ref, inv_high_ref, inv_low_ref, cross_high_ref, cross_low_ref, reduced_ref, x_ref):
    width = moment_ref.shape[1]
    start = 2 * PANEL
    x_ref[...] = x_in_ref[...]
    eliminate_blocks(x_ref, PANEL // TILE // 2, PANEL // TILE)
    inv_high_ref[...], inv_low_ref[...] = split(x_ref[:, PANEL:start].T)
    cross = x_ref[:, start : start + width]
    cross_high_ref[...], cross_low_ref[...] = split(cross)
    solved = x_ref[:, start + width : start + width + 1]
    reduced = moment_ref[...] / sample_count - jnp.sum(cross * solved, axis=0, keepdims=True)
    reduced_ref[...] = jnp.sqrt(jnp.float32(sample_count)) * reduced


def eliminate_front(shift, feat_panel, feat, moment_panel):
    count, width = feat.shape
    vmem = pl.BlockSpec(memory_space=pltpu.VMEM)
    return pl.pallas_call(
        functools.partial(front_kernel, count),
        in_specs=[pl.BlockSpec(memory_space=pltpu.SMEM)] + [vmem] * 3,
        out_specs=vmem,
        out_shape=jax.ShapeDtypeStruct((PANEL, 2 * PANEL + width + LANES), jnp.float32),
        cost_estimate=pl.CostEstimate(flops=20 * 10**9, bytes_accessed=8 * 10**6, transcendentals=0),
        compiler_params=pltpu.CompilerParams(vmem_limit_bytes=VMEM_BYTES),
    )(shift, feat_panel, feat, moment_panel)


def eliminate_back(count, state, moment):
    width = moment.shape[1]
    vmem = pl.BlockSpec(memory_space=pltpu.VMEM)
    square = jax.ShapeDtypeStruct((PANEL, PANEL), jnp.bfloat16)
    wide = jax.ShapeDtypeStruct((PANEL, width), jnp.bfloat16)
    return pl.pallas_call(
        functools.partial(back_kernel, count),
        in_specs=[vmem] * 2,
        out_specs=[vmem] * 5,
        out_shape=[square, square, wide, wide, jax.ShapeDtypeStruct((1, width), jnp.float32)],
        scratch_shapes=[pltpu.VMEM(state.shape, jnp.float32)],
        cost_estimate=pl.CostEstimate(flops=20 * 10**9, bytes_accessed=8 * 10**6, transcendentals=0),
        compiler_params=pltpu.CompilerParams(vmem_limit_bytes=VMEM_BYTES),
    )(state, moment)


def three_pass(left, right_high, right_low):
    high, low = split(left)
    dot = functools.partial(jnp.dot, preferred_element_type=jnp.float32)
    return dot(high, right_high) + (dot(high, right_low) + dot(low, right_high))


def main_kernel(
    sample_count,
    blocks,
    order_ref,
    place_ref,
    pos_ref,
    *refs,
):
    freq_refs = refs[:blocks]
    (
        emb_ref,
        treated_ref,
        feat_ref,
        feat_panel_ref,
        inv_high_ref,
        inv_low_ref,
        cross_high_ref,
        cross_low_ref,
        schur_ref,
        panel_ref,
        slots,
        sems,
    ) = refs[blocks:]
    now = pl.program_id(0)

    def fetch(index, slot):
        for k in range(blocks):

            @pl.when(index == k)
            def _():
                pltpu.make_async_copy(freq_refs[k], slots.at[slot], sems.at[slot]).start()

    @pl.when(now == 0)
    def _():
        fetch(0, 0)

    fetch(now + 1, lax.rem(now + 1, 2))
    slot = lax.rem(now, 2)
    pltpu.make_async_copy(freq_refs[0], slots.at[slot], sems.at[slot]).wait()

    height = slots.shape[1]
    count, emb_width = emb_ref.shape
    width = feat_ref.shape[1]
    parts = slots[slot, :, emb_width : emb_width + LANES].astype(jnp.float32)
    base = (parts[:, 0:1] + parts[:, 1:2]) + parts[:, 2:3]
    full = (parts[:, 3:4] + parts[:, 4:5]) + parts[:, 5:6]
    own = jnp.zeros((height, width), jnp.float32)
    panel = jnp.zeros((height, PANEL), jnp.float32)
    step = count // pos_ref.shape[0]
    for j in range(count // step):
        at = j * step
        emb = emb_ref[pl.ds(pl.multiple_of(pos_ref[j] * step, step), step), :]
        scaled = lax.dot_general(
            slots[slot, :, :emb_width], emb, (((1,), (1,)), ((), ())), preferred_element_type=jnp.float32
        )
        phase = jnp.where(treated_ref[:, at : at + step] > 0.5, full, base)
        features = cosine_turns(scaled * turn + phase).astype(jnp.bfloat16)
        own += jnp.dot(features, feat_ref[at : at + step, :], preferred_element_type=jnp.float32)
        panel += jnp.dot(features, feat_panel_ref[at : at + step, :], preferred_element_type=jnp.float32)
    first = place_ref[0] + order_ref[now] * height
    rows = first + lax.broadcasted_iota(jnp.int32, (height, width), 0)
    cols = place_ref[1] + lax.broadcasted_iota(jnp.int32, (height, width), 1)
    own = own / sample_count + jnp.where(rows == cols, ridge, 0.0)
    rows = first + lax.broadcasted_iota(jnp.int32, (height, PANEL), 0)
    cols = place_ref[2] + lax.broadcasted_iota(jnp.int32, (height, PANEL), 1)
    panel = panel / sample_count + jnp.where(rows == cols, ridge, 0.0)
    factor = three_pass(panel, inv_high_ref[...], inv_low_ref[...])
    panel_ref[...] = factor
    schur_ref[...] = own - three_pass(factor, cross_high_ref[...], cross_low_ref[...])


def main(order, place, pos, freqs, emb, treated, feat, feat_panel, solved):
    blocks = len(freqs)
    height = freqs[0].shape[0]
    row_height = blocks * height
    emb_width = emb.shape[1]
    count, width = feat.shape
    fixed = lambda array: pl.BlockSpec(array.shape, lambda i, *_: (0, 0), pipeline_mode=pl.Buffered(1))
    moved = lambda cols: pl.BlockSpec((height, cols), lambda i, order, *_: (order[i], 0))
    flops = 2 * row_height * (count * (emb_width + width + PANEL) + 3 * PANEL * (PANEL + width))
    return pl.pallas_call(
        functools.partial(main_kernel, count, blocks),
        grid_spec=pltpu.PrefetchScalarGridSpec(
            num_scalar_prefetch=3,
            grid=(blocks,),
            in_specs=[pl.BlockSpec(memory_space=pl.ANY)] * blocks
            + [fixed(array) for array in (emb, treated, feat, feat_panel, *solved)],
            out_specs=[moved(width), moved(PANEL)],
            scratch_shapes=[
                pltpu.VMEM((2, height, freqs[0].shape[1]), jnp.bfloat16),
                pltpu.SemaphoreType.DMA((2,)),
            ],
        ),
        out_shape=[
            jax.ShapeDtypeStruct((row_height, width), jnp.float32),
            jax.ShapeDtypeStruct((row_height, PANEL), jnp.float32),
        ],
        cost_estimate=pl.CostEstimate(flops=flops, bytes_accessed=30 * 10**6, transcendentals=count * row_height),
        compiler_params=pltpu.CompilerParams(vmem_limit_bytes=VMEM_BYTES),
    )(order, place, pos, *freqs, emb, treated, feat, feat_panel, *solved)


def spread_kernel(axis_size, x_ref, out_ref, sums, arrived, send_sems, recv_sems):
    samp, feat = lax.axis_index("samp"), lax.axis_index("feat")
    rows = x_ref.shape[0]
    bits = []
    while (1 << len(bits)) < axis_size:
        bits.append(1 << len(bits))
    sides = [(feat // bit) % 2 for bit in bits]
    mates = [feat + bit * (1 - 2 * side) for bit, side in zip(bits, sides)]

    barrier = pltpu.get_barrier_semaphore()
    for mate in mates:
        pl.semaphore_signal(barrier, inc=1, device_id=(samp, mate), device_id_type=pl.DeviceIdType.MESH)
    pl.semaphore_wait(barrier, len(bits))

    def send(source, target, mate, index):
        copy = pltpu.make_async_remote_copy(
            src_ref=source,
            dst_ref=target,
            send_sem=send_sems.at[index],
            recv_sem=recv_sems.at[index],
            device_id=(samp, mate),
            device_id_type=pl.DeviceIdType.MESH,
        )
        copy.start()
        copy.wait()

    first = 0
    firsts = []
    size = rows
    source = x_ref
    landing = 0
    for index, (side, mate) in enumerate(zip(sides, mates)):
        size //= 2
        kept = pl.multiple_of(first + side * size, 16)
        given = pl.multiple_of(first + (1 - side) * size, 16)
        place = pl.ds(landing, size)
        send(source.at[pl.ds(given, size)], arrived.at[place], mate, index)
        total = source[pl.ds(kept, size), :] + arrived[place, :]
        landing += size
        first = kept
        firsts.append((first, size))
        if index < len(bits) - 1:
            sums[pl.ds(kept, size), :] = total
            source = sums
        else:
            out_ref[pl.ds(kept, size), :] = total
    for index in reversed(range(len(bits))):
        first, size = firsts[index]
        part = out_ref.at[pl.ds(first, size)]
        send(part, part, mates[index], len(bits) + index)


def spread(x):
    axis_size = lax.axis_size("feat")
    steps = 2 * (axis_size.bit_length() - 1)
    return pl.pallas_call(
        functools.partial(spread_kernel, axis_size),
        in_specs=[pl.BlockSpec(memory_space=pltpu.VMEM)],
        out_specs=pl.BlockSpec(memory_space=pltpu.VMEM),
        out_shape=jax.ShapeDtypeStruct(x.shape, x.dtype),
        scratch_shapes=[
            pltpu.VMEM(x.shape, x.dtype),
            pltpu.VMEM(x.shape, x.dtype),
            pltpu.SemaphoreType.DMA((steps,)),
            pltpu.SemaphoreType.DMA((steps,)),
        ],
        cost_estimate=pl.CostEstimate(flops=45 * 10**9, bytes_accessed=2 * 10**6, transcendentals=0),
        compiler_params=pltpu.CompilerParams(collective_id=0, has_side_effects=True, vmem_limit_bytes=16 * 1024 * 1024),
    )(x)


def swap(value, bits):
    return lax.ppermute(value, "feat", [(f, f ^ bits) for f in range(lax.axis_size("feat"))])


def gather_samples_staged(embeddings, marks, samp_index, feat_index):
    part = embeddings.shape[0] // 2
    core = feat_index % 2
    mine = lax.dynamic_slice_in_dim(embeddings, core * part, part, 0)
    got = lax.ppermute(mine, "samp", [(0, 1), (1, 0)])
    other_marks = lax.ppermute(marks, "samp", [(0, 1), (1, 0)])
    emb = jnp.concatenate([embeddings, got, swap(got, 1)], axis=0)
    piece = jnp.arange(4, dtype=jnp.int32)
    pos = jnp.where(piece // 2 == samp_index, piece % 2, jnp.where(piece % 2 == core, 2, 3))
    first = samp_index == 0
    marks = jnp.concatenate([jnp.where(first, marks, other_marks), jnp.where(first, other_marks, marks)], axis=1)
    return emb, marks, pos.astype(jnp.int32)


def per_device(embeddings, frequencies, phases, treat_freq, treatment, flips, panel):
    samp_size = lax.axis_size("samp")
    feat_size = lax.axis_size("feat")
    samp_index = lax.axis_index("samp")
    feat_index = lax.axis_index("feat")
    emb_width, col_width = frequencies.shape
    feat_total = col_width * feat_size
    row_height = feat_total // samp_size
    first_col = panel[0] * PANEL
    first_dev = first_col // col_width
    staged = samp_size == 2 and feat_size == 16 and col_width == PANEL
    half = 8

    base = phases * turn
    parts = jnp.stack(thirds(base) + thirds(base + treat_freq * turn))
    freq_t = jnp.concatenate([frequencies.T, jnp.pad(parts.T, ((0, 0), (0, LANES - 6)))], axis=1)

    treated = treatment.astype(jnp.float32)
    flipped = flips.astype(jnp.float32)
    counter = treated + flipped - 2.0 * treated * flipped
    marks = jnp.stack([treated, counter])
    if staged:
        emb, marks, pos = gather_samples_staged(embeddings, marks, samp_index, feat_index)
        mates = [(s * 16 + f, s * 16 + (f ^ half)) for s in range(2) for f in range(s * half, (s + 1) * half)]
        crossed = lax.ppermute(freq_t, ("samp", "feat"), mates)
        mine = jnp.where(feat_index // half == samp_index, freq_t, crossed)
    else:
        emb = lax.all_gather(embeddings, "samp", axis=0, tiled=True)
        marks = lax.all_gather(marks, "samp", axis=1, tiled=True)
        pos = jnp.arange(emb.shape[0] // 512, dtype=jnp.int32)

    if staged:
        panel_freq = spread(jnp.where(feat_index == first_dev, freq_t, jnp.zeros_like(freq_t)))
    else:
        panel_freq = []
        for member in range(PANEL // col_width):
            own = feat_index == first_dev + member
            panel_freq.append(lax.psum(jnp.where(own, freq_t, jnp.zeros_like(freq_t)), "feat"))
        panel_freq = jnp.concatenate(panel_freq, axis=0)

    treated_col, counter_col = marks[0][:, None], marks[1][:, None]
    feat, moment = make_features(pos, emb, freq_t, treated_col, counter_col)
    if staged:
        mine, panel_freq, feat = lax.optimization_barrier((mine, panel_freq, feat))
        near = [swap(mine, 4), swap(mine, 2), swap(mine, 6)]
    feat_panel, moment_panel = make_features(pos, emb, panel_freq, treated_col, counter_col)
    own_col = feat_index * col_width
    shift = (own_col - first_col).reshape(1).astype(jnp.int32)
    state = eliminate_front(shift, feat_panel, feat, moment_panel)
    if staged:
        state, near = lax.optimization_barrier((state, near))
        near = [mine] + near
        freqs = near + [swap(block, 1) for block in near]
        order = jnp.bitwise_xor(feat_index % half, jnp.array([0, 4, 2, 6, 1, 5, 3, 7], jnp.int32))
    else:
        rows = lax.all_gather(freq_t, "feat", axis=0, tiled=True)
        rows = lax.dynamic_slice_in_dim(rows, samp_index * row_height, row_height, 0)
        freqs = jnp.split(rows, row_height // col_width, axis=0)
        order = jnp.arange(row_height // col_width, dtype=jnp.int32)
    *solved, reduced = eliminate_back(emb.shape[0], state, moment)
    place = jnp.stack([samp_index * row_height, own_col, first_col]).astype(jnp.int32)
    schur, panel_factor = main(order, place, pos, freqs, emb, marks[:1], feat, feat_panel, solved)
    return schur, panel_factor, reduced[0]


def solution(mesh):
    return jax.shard_map(
        per_device,
        mesh=mesh,
        in_specs=(
            P("samp", None),
            P(None, "feat"),
            P("feat"),
            P("feat"),
            P("samp"),
            P("samp"),
            P(),
        ),
        out_specs=(P("samp", "feat"), P("samp", None), P("feat")),
        check_vma=False,
    )
```

```python
import functools

import jax
import jax.numpy as jnp
from jax import lax
from jax.experimental import pallas as pl
from jax.experimental.pallas import tpu as pltpu
from jax.sharding import PartitionSpec as P

PANEL = 512
TILE = 128
LANES = 128

ridge = 0.1
turn = 0.15915494309189535
magic = 12582912.0
VMEM_BYTES = 58 * 1024 * 1024
COS = (1.4142124462507522, -27.915133726537626, 91.8229879115028, -120.59228365935401, 83.14231129485714, -29.79904335273614)


def cosine_turns(u):
    whole = (u + magic) - magic
    frac = u - whole
    square = frac * frac
    acc = jnp.full_like(square, COS[-1])
    for coef in COS[-2::-1]:
        acc = acc * square + coef
    return acc


def split(value):
    high = value.astype(jnp.bfloat16)
    return high, (value - high.astype(jnp.float32)).astype(jnp.bfloat16)


def thirds(value):
    high = lax.reduce_precision(value, 8, 7)
    middle = lax.reduce_precision(value - high, 8, 7)
    low = value - high - middle
    return [part.astype(jnp.bfloat16) for part in (high, middle, low)]


def feature_kernel(pos_ref, emb_ref, freq_ref, treated_ref, counter_ref, feat_ref, moment_ref):
    @pl.when(pl.program_id(0) == 0)
    def _():
        moment_ref[...] = jnp.zeros_like(moment_ref)

    width = emb_ref.shape[1]
    parts = freq_ref[:, width:].astype(jnp.float32).T
    base = (parts[0:1] + parts[1:2]) + parts[2:3]
    full = (parts[3:4] + parts[4:5]) + parts[5:6]
    scaled = lax.dot_general(
        emb_ref[...], freq_ref[:, :width], (((1,), (1,)), ((), ())), preferred_element_type=jnp.float32
    ) * turn
    observed = cosine_turns(scaled + jnp.where(treated_ref[...] > 0.5, full, base))
    counterfactual = cosine_turns(scaled + jnp.where(counter_ref[...] > 0.5, full, base))
    feat_ref[...] = observed.astype(jnp.bfloat16)
    moment_ref[...] += jnp.sum(counterfactual - observed, axis=0, keepdims=True)


def make_features(pos, emb, freq, treated, counter):
    count, emb_width = emb.shape
    width = freq.shape[0]
    step = 256
    ratio = count // pos.shape[0] // step
    whole = lambda shape: pl.BlockSpec(shape, lambda i, pos: (0, 0))
    return pl.pallas_call(
        feature_kernel,
        grid_spec=pltpu.PrefetchScalarGridSpec(
            num_scalar_prefetch=1,
            grid=(count // step,),
            in_specs=[
                pl.BlockSpec((step, emb_width), lambda i, pos: (pos[i // ratio] * ratio + i % ratio, 0)),
                whole(freq.shape),
                pl.BlockSpec((step, 1), lambda i, pos: (i, 0)),
                pl.BlockSpec((step, 1), lambda i, pos: (i, 0)),
            ],
            out_specs=[pl.BlockSpec((step, width), lambda i, pos: (i, 0)), whole((1, width))],
        ),
        out_shape=[
            jax.ShapeDtypeStruct((count, width), jnp.bfloat16),
            jax.ShapeDtypeStruct((1, width), jnp.float32),
        ],
        cost_estimate=pl.CostEstimate(
            flops=2 * count * emb_width * width, bytes_accessed=2 * count * emb_width, transcendentals=2 * count * width
        ),
        compiler_params=pltpu.CompilerParams(vmem_limit_bytes=VMEM_BYTES),
    )(pos, emb, freq, treated, counter)


def inverse_factor(tile):
    groups = TILE // 8
    at_once = 4
    sub = lax.broadcasted_iota(jnp.int32, (8, TILE), 0)
    lane = lax.broadcasted_iota(jnp.int32, (8, TILE), 1)
    left = [tile[8 * g : 8 * g + 8, :] for g in range(groups)]
    right = [jnp.where(lane == sub + 8 * g, 1.0, 0.0) for g in range(groups)]
    spread = lambda value: jnp.broadcast_to(value, (8, TILE))
    for j in range(0, TILE, at_once):
        g, t = divmod(j, 8)
        ks = range(at_once)
        rows = [spread(left[g][t + k : t + k + 1, :]) for k in ks]
        marks = [spread(right[g][t + k : t + k + 1, :]) for k in ks]
        p = {(k, m): spread(rows[k][:, j + m : j + m + 1]) for k in ks for m in range(k, at_once)}
        f, inv = {}, []
        for k in ks:
            inv.append(1.0 / p[k, k])
            for m in range(k + 1, at_once):
                f[m, k] = p[k, m] * inv[k]
            for m in range(k + 1, at_once):
                for n in range(m, at_once):
                    p[m, n] = p[m, n] - f[m, k] * p[k, n]
        for k in ks:
            for q in range(k):
                rows[k] = rows[k] - f[k, q] * rows[q]
                marks[k] = marks[k] - f[k, q] * marks[q]
        row_part, mark_part = [None] * at_once, [None] * at_once
        for k in reversed(ks):
            row_part[k] = rows[k] * inv[k]
            mark_part[k] = marks[k] * inv[k]
            for q in range(k + 1, at_once):
                row_part[k] = row_part[k] - f[q, k] * row_part[q]
                mark_part[k] = mark_part[k] - f[q, k] * mark_part[q]
        for i in range(g, groups):
            if i > g or t + at_once < 8:
                cols = [spread(left[i][:, j + k : j + k + 1]) for k in ks]
                if i == g:
                    cols = [jnp.where(sub >= t + at_once, col, 0.0) for col in cols]
                left_sum = (cols[0] * row_part[0] + cols[1] * row_part[1]) + (cols[2] * row_part[2] + cols[3] * row_part[3])
                right_sum = (cols[0] * mark_part[0] + cols[1] * mark_part[1]) + (cols[2] * mark_part[2] + cols[3] * mark_part[3])
                left[i] = left[i] - left_sum
                right[i] = right[i] - right_sum
        for k in ks:
            left[g] = jnp.where(sub == t + k, rows[k], left[g])
            right[g] = jnp.where(sub == t + k, marks[k], right[g])
    out = []
    for g in range(groups):
        diag = jnp.sum(jnp.where(lane == sub + 8 * g, left[g], 0.0), axis=1, keepdims=True)
        out.append(right[g] * (1.0 / jnp.sqrt(diag)))
    return jnp.concatenate(out, axis=0)


def eliminate_blocks(x_ref, first, last):
    def block(b, carry):
        at = pl.multiple_of(b * TILE, TILE)
        inverse = inverse_factor(x_ref[pl.ds(at, TILE), pl.ds(at, TILE)])
        solved = jnp.dot(inverse, x_ref[pl.ds(at, TILE), :], precision=lax.Precision.HIGHEST, preferred_element_type=jnp.float32)
        lanes = lax.broadcasted_iota(jnp.int32, (TILE, PANEL), 1)

        @pl.when(b < PANEL // TILE - 1)
        def _():
            coef = jnp.where(lanes >= at + TILE, solved[:, :PANEL], 0.0)
            x_ref[...] -= jnp.dot(coef.T, solved, precision=lax.Precision.HIGHEST, preferred_element_type=jnp.float32)

        x_ref[pl.ds(at, TILE), :] = solved
        return carry

    lax.fori_loop(first, last, block, 0)


def front_kernel(sample_count, shift_ref, feat_panel_ref, feat_ref, moment_panel_ref, x_ref):
    width = feat_ref.shape[1]
    start = 2 * PANEL
    panel_t = feat_panel_ref[...].T
    dot = functools.partial(jnp.dot, preferred_element_type=jnp.float32)
    rows = lax.broadcasted_iota(jnp.int32, (PANEL, PANEL), 0)
    cols = lax.broadcasted_iota(jnp.int32, (PANEL, PANEL), 1)
    eye = jnp.where(rows == cols, 1.0, 0.0)
    x_ref[:, 0:PANEL] = dot(panel_t, feat_panel_ref[...]) / sample_count + ridge * eye
    x_ref[:, PANEL:start] = eye
    rows = lax.broadcasted_iota(jnp.int32, (PANEL, width), 0)
    cols = lax.broadcasted_iota(jnp.int32, (PANEL, width), 1)
    own = jnp.where(rows == cols + shift_ref[0], ridge, 0.0)
    x_ref[:, start : start + width] = dot(panel_t, feat_ref[...]) / sample_count + own
    column = jnp.sum(eye * (moment_panel_ref[...] / sample_count), axis=1, keepdims=True)
    x_ref[:, start + width :] = jnp.broadcast_to(column, (PANEL, LANES))
    eliminate_blocks(x_ref, 0, PANEL // TILE // 2)


def back_kernel(sample_count, x_in_ref, moment_ref, inv_high_ref, inv_low_ref, cross_high_ref, cross_low_ref, reduced_ref, x_ref):
    width = moment_ref.shape[1]
    start = 2 * PANEL
    x_ref[...] = x_in_ref[...]
    eliminate_blocks(x_ref, PANEL // TILE // 2, PANEL // TILE)
    inv_high_ref[...], inv_low_ref[...] = split(x_ref[:, PANEL:start].T)
    cross = x_ref[:, start : start + width]
    cross_high_ref[...], cross_low_ref[...] = split(cross)
    solved = x_ref[:, start + width : start + width + 1]
    reduced = moment_ref[...] / sample_count - jnp.sum(cross * solved, axis=0, keepdims=True)
    reduced_ref[...] = jnp.sqrt(jnp.float32(sample_count)) * reduced


def eliminate_front(shift, feat_panel, feat, moment_panel):
    count, width = feat.shape
    vmem = pl.BlockSpec(memory_space=pltpu.VMEM)
    return pl.pallas_call(
        functools.partial(front_kernel, count),
        in_specs=[pl.BlockSpec(memory_space=pltpu.SMEM)] + [vmem] * 3,
        out_specs=vmem,
        out_shape=jax.ShapeDtypeStruct((PANEL, 2 * PANEL + width + LANES), jnp.float32),
        cost_estimate=pl.CostEstimate(flops=20 * 10**9, bytes_accessed=8 * 10**6, transcendentals=0),
        compiler_params=pltpu.CompilerParams(vmem_limit_bytes=VMEM_BYTES),
    )(shift, feat_panel, feat, moment_panel)


def eliminate_back(count, state, moment):
    width = moment.shape[1]
    vmem = pl.BlockSpec(memory_space=pltpu.VMEM)
    square = jax.ShapeDtypeStruct((PANEL, PANEL), jnp.bfloat16)
    wide = jax.ShapeDtypeStruct((PANEL, width), jnp.bfloat16)
    return pl.pallas_call(
        functools.partial(back_kernel, count),
        in_specs=[vmem] * 2,
        out_specs=[vmem] * 5,
        out_shape=[square, square, wide, wide, jax.ShapeDtypeStruct((1, width), jnp.float32)],
        scratch_shapes=[pltpu.VMEM(state.shape, jnp.float32)],
        cost_estimate=pl.CostEstimate(flops=20 * 10**9, bytes_accessed=8 * 10**6, transcendentals=0),
        compiler_params=pltpu.CompilerParams(vmem_limit_bytes=VMEM_BYTES),
    )(state, moment)


def three_pass(left, right_high, right_low):
    high, low = split(left)
    dot = functools.partial(jnp.dot, preferred_element_type=jnp.float32)
    return dot(high, right_high) + (dot(high, right_low) + dot(low, right_high))


def main_kernel(
    sample_count,
    blocks,
    order_ref,
    place_ref,
    pos_ref,
    *refs,
):
    freq_refs = refs[:blocks]
    (
        emb_ref,
        treated_ref,
        feat_ref,
        feat_panel_ref,
        inv_high_ref,
        inv_low_ref,
        cross_high_ref,
        cross_low_ref,
        schur_ref,
        panel_ref,
        slots,
        sems,
    ) = refs[blocks:]
    now = pl.program_id(0)

    def fetch(index, slot):
        for k in range(blocks):

            @pl.when(index == k)
            def _():
                pltpu.make_async_copy(freq_refs[k], slots.at[slot], sems.at[slot]).start()

    @pl.when(now == 0)
    def _():
        fetch(0, 0)

    fetch(now + 1, lax.rem(now + 1, 2))
    slot = lax.rem(now, 2)
    pltpu.make_async_copy(freq_refs[0], slots.at[slot], sems.at[slot]).wait()

    height = slots.shape[1]
    count, emb_width = emb_ref.shape
    width = feat_ref.shape[1]
    parts = slots[slot, :, emb_width : emb_width + LANES].astype(jnp.float32)
    base = (parts[:, 0:1] + parts[:, 1:2]) + parts[:, 2:3]
    full = (parts[:, 3:4] + parts[:, 4:5]) + parts[:, 5:6]
    own = jnp.zeros((height, width), jnp.float32)
    panel = jnp.zeros((height, PANEL), jnp.float32)
    step = count // pos_ref.shape[0]
    for j in range(count // step):
        at = j * step
        emb = emb_ref[pl.ds(pl.multiple_of(pos_ref[j] * step, step), step), :]
        scaled = lax.dot_general(
            slots[slot, :, :emb_width], emb, (((1,), (1,)), ((), ())), preferred_element_type=jnp.float32
        )
        phase = jnp.where(treated_ref[:, at : at + step] > 0.5, full, base)
        features = cosine_turns(scaled * turn + phase).astype(jnp.bfloat16)
        own += jnp.dot(features, feat_ref[at : at + step, :], preferred_element_type=jnp.float32)
        panel += jnp.dot(features, feat_panel_ref[at : at + step, :], preferred_element_type=jnp.float32)
    first = place_ref[0] + order_ref[now] * height
    rows = first + lax.broadcasted_iota(jnp.int32, (height, width), 0)
    cols = place_ref[1] + lax.broadcasted_iota(jnp.int32, (height, width), 1)
    own = own / sample_count + jnp.where(rows == cols, ridge, 0.0)
    rows = first + lax.broadcasted_iota(jnp.int32, (height, PANEL), 0)
    cols = place_ref[2] + lax.broadcasted_iota(jnp.int32, (height, PANEL), 1)
    panel = panel / sample_count + jnp.where(rows == cols, ridge, 0.0)
    factor = three_pass(panel, inv_high_ref[...], inv_low_ref[...])
    panel_ref[...] = factor
    schur_ref[...] = own - three_pass(factor, cross_high_ref[...], cross_low_ref[...])


def main(order, place, pos, freqs, emb, treated, feat, feat_panel, solved):
    blocks = len(freqs)
    height = freqs[0].shape[0]
    row_height = blocks * height
    emb_width = emb.shape[1]
    count, width = feat.shape
    fixed = lambda array: pl.BlockSpec(array.shape, lambda i, *_: (0, 0), pipeline_mode=pl.Buffered(1))
    moved = lambda cols: pl.BlockSpec((height, cols), lambda i, order, *_: (order[i], 0))
    flops = 2 * row_height * (count * (emb_width + width + PANEL) + 3 * PANEL * (PANEL + width))
    return pl.pallas_call(
        functools.partial(main_kernel, count, blocks),
        grid_spec=pltpu.PrefetchScalarGridSpec(
            num_scalar_prefetch=3,
            grid=(blocks,),
            in_specs=[pl.BlockSpec(memory_space=pl.ANY)] * blocks
            + [fixed(array) for array in (emb, treated, feat, feat_panel, *solved)],
            out_specs=[moved(width), moved(PANEL)],
            scratch_shapes=[
                pltpu.VMEM((2, height, freqs[0].shape[1]), jnp.bfloat16),
                pltpu.SemaphoreType.DMA((2,)),
            ],
        ),
        out_shape=[
            jax.ShapeDtypeStruct((row_height, width), jnp.float32),
            jax.ShapeDtypeStruct((row_height, PANEL), jnp.float32),
        ],
        cost_estimate=pl.CostEstimate(flops=flops, bytes_accessed=30 * 10**6, transcendentals=count * row_height),
        compiler_params=pltpu.CompilerParams(vmem_limit_bytes=VMEM_BYTES),
    )(order, place, pos, *freqs, emb, treated, feat, feat_panel, *solved)


def entry_kernel(
    axis_size, x_ref, freq_ref, emb_ref, out_ref, mine_ref, all_ref, sums, arrived, send_sems, recv_sems, local_sems
):
    samp, feat = lax.axis_index("samp"), lax.axis_index("feat")
    rows = x_ref.shape[0]
    bits = []
    while (1 << len(bits)) < axis_size:
        bits.append(1 << len(bits))
    sides = [(feat // bit) % 2 for bit in bits]
    mates = [feat + bit * (1 - 2 * side) for bit, side in zip(bits, sides)]

    barrier = pltpu.get_barrier_semaphore()
    for mate in mates:
        pl.semaphore_signal(barrier, inc=1, device_id=(samp, mate), device_id_type=pl.DeviceIdType.MESH)
    pl.semaphore_signal(barrier, inc=1, device_id=(1 - samp, feat), device_id_type=pl.DeviceIdType.MESH)
    pl.semaphore_wait(barrier, len(bits) + 1)

    def remote(source, target, device, index):
        return pltpu.make_async_remote_copy(
            src_ref=source,
            dst_ref=target,
            send_sem=send_sems.at[index],
            recv_sem=recv_sems.at[index],
            device_id=device,
            device_id_type=pl.DeviceIdType.MESH,
        )

    def send(source, target, mate, index):
        copy = remote(source, target, (samp, mate), index)
        copy.start()
        copy.wait()

    steps = 2 * len(bits)
    count = emb_ref.shape[0]
    part_rows = count // 2
    core = feat % 2
    mine_at = pl.multiple_of(samp * count + core * part_rows, 16)
    other_at = pl.multiple_of((1 - samp) * count + core * part_rows, 16)
    across = remote(
        emb_ref.at[pl.ds(pl.multiple_of(core * part_rows, 16), part_rows)],
        all_ref.at[pl.ds(mine_at, part_rows)],
        (1 - samp, feat),
        steps,
    )
    across.start()
    keeps = feat // (axis_size // 2) == samp
    crossing = remote(freq_ref, mine_ref, (samp, mates[-1]), steps + 1)
    keep = pltpu.make_async_copy(freq_ref, mine_ref, local_sems.at[0])
    stay = pltpu.make_async_copy(
        emb_ref, all_ref.at[pl.ds(pl.multiple_of(samp * count, 16), count)], local_sems.at[1]
    )

    @pl.when(keeps)
    def _():
        crossing.start()
        keep.start()

    stay.start()

    first = 0
    firsts = []
    size = rows
    source = x_ref
    landing = 0
    for index, (side, mate) in enumerate(zip(sides, mates)):
        size //= 2
        kept = pl.multiple_of(first + side * size, 16)
        given = pl.multiple_of(first + (1 - side) * size, 16)
        place = pl.ds(landing, size)
        send(source.at[pl.ds(given, size)], arrived.at[place], mate, index)
        total = source[pl.ds(kept, size), :] + arrived[place, :]
        landing += size
        first = kept
        firsts.append((first, size))
        if index < len(bits) - 1:
            sums[pl.ds(kept, size), :] = total
            source = sums
        else:
            out_ref[pl.ds(kept, size), :] = total
    for index in reversed(range(len(bits))):
        first, size = firsts[index]
        part = out_ref.at[pl.ds(first, size)]
        send(part, part, mates[index], len(bits) + index)
    across.wait()
    fetched = all_ref.at[pl.ds(other_at, part_rows)]
    forward = remote(fetched, fetched, (samp, mates[0]), steps + 2)
    forward.start()
    forward.wait()
    stay.wait()

    @pl.when(keeps)
    def _():
        crossing.wait_send()
        keep.wait()

    @pl.when(jnp.logical_not(keeps))
    def _():
        crossing.wait_recv()


def enter(x, freq_t, emb):
    axis_size = lax.axis_size("feat")
    steps = 2 * (axis_size.bit_length() - 1) + 3
    vmem, anywhere = pl.BlockSpec(memory_space=pltpu.VMEM), pl.BlockSpec(memory_space=pl.ANY)
    return pl.pallas_call(
        functools.partial(entry_kernel, axis_size),
        in_specs=[vmem, anywhere, anywhere],
        out_specs=[vmem, anywhere, anywhere],
        out_shape=[
            jax.ShapeDtypeStruct(x.shape, x.dtype),
            jax.ShapeDtypeStruct(freq_t.shape, freq_t.dtype),
            jax.ShapeDtypeStruct((2 * emb.shape[0], emb.shape[1]), emb.dtype),
        ],
        scratch_shapes=[
            pltpu.VMEM(x.shape, x.dtype),
            pltpu.VMEM(x.shape, x.dtype),
            pltpu.SemaphoreType.DMA((steps,)),
            pltpu.SemaphoreType.DMA((steps,)),
            pltpu.SemaphoreType.DMA((2,)),
        ],
        cost_estimate=pl.CostEstimate(flops=45 * 10**9, bytes_accessed=2 * 10**6, transcendentals=0),
        compiler_params=pltpu.CompilerParams(collective_id=0, has_side_effects=True, vmem_limit_bytes=16 * 1024 * 1024),
    )(x, freq_t, emb)


def swap(value, bits):
    return lax.ppermute(value, "feat", [(f, f ^ bits) for f in range(lax.axis_size("feat"))])


def per_device(embeddings, frequencies, phases, treat_freq, treatment, flips, panel):
    samp_size = lax.axis_size("samp")
    feat_size = lax.axis_size("feat")
    samp_index = lax.axis_index("samp")
    feat_index = lax.axis_index("feat")
    emb_width, col_width = frequencies.shape
    feat_total = col_width * feat_size
    row_height = feat_total // samp_size
    first_col = panel[0] * PANEL
    first_dev = first_col // col_width
    staged = samp_size == 2 and feat_size == 16 and col_width == PANEL
    half = 8

    base = phases * turn
    parts = jnp.stack(thirds(base) + thirds(base + treat_freq * turn))
    freq_t = jnp.concatenate([frequencies.T, jnp.pad(parts.T, ((0, 0), (0, LANES - 6)))], axis=1)

    treated = treatment.astype(jnp.float32)
    flipped = flips.astype(jnp.float32)
    counter = treated + flipped - 2.0 * treated * flipped
    marks = jnp.stack([treated, counter])
    if staged:
        masked = jnp.where(feat_index == first_dev, freq_t, jnp.zeros_like(freq_t))
        other_marks = lax.ppermute(marks, "samp", [(0, 1), (1, 0)])
        first = samp_index == 0
        marks = jnp.concatenate([jnp.where(first, marks, other_marks), jnp.where(first, other_marks, marks)], axis=1)
        panel_freq, mine, emb = enter(masked, freq_t, embeddings)
        near = [swap(mine, 4), swap(mine, 2), swap(mine, 6)]
    else:
        emb = lax.all_gather(embeddings, "samp", axis=0, tiled=True)
        marks = lax.all_gather(marks, "samp", axis=1, tiled=True)
        panel_freq = []
        for member in range(PANEL // col_width):
            own = feat_index == first_dev + member
            panel_freq.append(lax.psum(jnp.where(own, freq_t, jnp.zeros_like(freq_t)), "feat"))
        panel_freq = jnp.concatenate(panel_freq, axis=0)
    pos = jnp.arange(emb.shape[0] // 512, dtype=jnp.int32)

    treated_col, counter_col = marks[0][:, None], marks[1][:, None]
    feat, moment = make_features(pos, emb, freq_t, treated_col, counter_col)
    feat_panel, moment_panel = make_features(pos, emb, panel_freq, treated_col, counter_col)
    own_col = feat_index * col_width
    shift = (own_col - first_col).reshape(1).astype(jnp.int32)
    state = eliminate_front(shift, feat_panel, feat, moment_panel)
    if staged:
        state, near = lax.optimization_barrier((state, near))
        near = [mine] + near
        freqs = near + [swap(block, 1) for block in near]
        order = jnp.bitwise_xor(feat_index % half, jnp.array([0, 4, 2, 6, 1, 5, 3, 7], jnp.int32))
    else:
        rows = lax.all_gather(freq_t, "feat", axis=0, tiled=True)
        rows = lax.dynamic_slice_in_dim(rows, samp_index * row_height, row_height, 0)
        freqs = jnp.split(rows, row_height // col_width, axis=0)
        order = jnp.arange(row_height // col_width, dtype=jnp.int32)
    *solved, reduced = eliminate_back(emb.shape[0], state, moment)
    place = jnp.stack([samp_index * row_height, own_col, first_col]).astype(jnp.int32)
    schur, panel_factor = main(order, place, pos, freqs, emb, marks[:1], feat, feat_panel, solved)
    return schur, panel_factor, reduced[0]


def solution(mesh):
    return jax.shard_map(
        per_device,
        mesh=mesh,
        in_specs=(
            P("samp", None),
            P(None, "feat"),
            P("feat"),
            P("feat"),
            P("samp"),
            P("samp"),
            P(),
        ),
        out_specs=(P("samp", "feat"), P("samp", None), P("feat")),
        check_vma=False,
    )
```

```python
import functools

import jax
import jax.numpy as jnp
from jax import lax
from jax.experimental import pallas as pl
from jax.experimental.pallas import tpu as pltpu
from jax.sharding import PartitionSpec as P

PANEL = 512
TILE = 128
LANES = 128

ridge = 0.1
turn = 0.15915494309189535
magic = 12582912.0
VMEM_BYTES = 58 * 1024 * 1024
COS = (1.4142124462507522, -27.915133726537626, 91.8229879115028, -120.59228365935401, 83.14231129485714, -29.79904335273614)


def cosine_turns(u):
    whole = (u + magic) - magic
    frac = u - whole
    square = frac * frac
    acc = jnp.full_like(square, COS[-1])
    for coef in COS[-2::-1]:
        acc = acc * square + coef
    return acc


def split(value):
    high = value.astype(jnp.bfloat16)
    return high, (value - high.astype(jnp.float32)).astype(jnp.bfloat16)


def thirds(value):
    high = lax.reduce_precision(value, 8, 7)
    middle = lax.reduce_precision(value - high, 8, 7)
    low = value - high - middle
    return [part.astype(jnp.bfloat16) for part in (high, middle, low)]


def feature_kernel(pos_ref, emb_ref, freq_ref, treated_ref, counter_ref, feat_ref, moment_ref):
    @pl.when(pl.program_id(0) == 0)
    def _():
        moment_ref[...] = jnp.zeros_like(moment_ref)

    width = emb_ref.shape[1]
    parts = freq_ref[:, width:].astype(jnp.float32).T
    base = (parts[0:1] + parts[1:2]) + parts[2:3]
    full = (parts[3:4] + parts[4:5]) + parts[5:6]
    scaled = lax.dot_general(
        emb_ref[...], freq_ref[:, :width], (((1,), (1,)), ((), ())), preferred_element_type=jnp.float32
    ) * turn
    observed = cosine_turns(scaled + jnp.where(treated_ref[...] > 0.5, full, base))
    counterfactual = cosine_turns(scaled + jnp.where(counter_ref[...] > 0.5, full, base))
    feat_ref[...] = observed.astype(jnp.bfloat16)
    moment_ref[...] += jnp.sum(counterfactual - observed, axis=0, keepdims=True)


def make_features(pos, emb, freq, treated, counter):
    count, emb_width = emb.shape
    width = freq.shape[0]
    step = 256
    ratio = count // pos.shape[0] // step
    whole = lambda shape: pl.BlockSpec(shape, lambda i, pos: (0, 0))
    return pl.pallas_call(
        feature_kernel,
        grid_spec=pltpu.PrefetchScalarGridSpec(
            num_scalar_prefetch=1,
            grid=(count // step,),
            in_specs=[
                pl.BlockSpec((step, emb_width), lambda i, pos: (pos[i // ratio] * ratio + i % ratio, 0)),
                whole(freq.shape),
                pl.BlockSpec((step, 1), lambda i, pos: (i, 0)),
                pl.BlockSpec((step, 1), lambda i, pos: (i, 0)),
            ],
            out_specs=[pl.BlockSpec((step, width), lambda i, pos: (i, 0)), whole((1, width))],
        ),
        out_shape=[
            jax.ShapeDtypeStruct((count, width), jnp.bfloat16),
            jax.ShapeDtypeStruct((1, width), jnp.float32),
        ],
        cost_estimate=pl.CostEstimate(
            flops=2 * count * emb_width * width, bytes_accessed=2 * count * emb_width, transcendentals=2 * count * width
        ),
        compiler_params=pltpu.CompilerParams(vmem_limit_bytes=VMEM_BYTES),
    )(pos, emb, freq, treated, counter)


def inverse_factor(tile):
    groups = TILE // 8
    at_once = 4
    sub = lax.broadcasted_iota(jnp.int32, (8, TILE), 0)
    lane = lax.broadcasted_iota(jnp.int32, (8, TILE), 1)
    left = [tile[8 * g : 8 * g + 8, :] for g in range(groups)]
    right = [jnp.where(lane == sub + 8 * g, 1.0, 0.0) for g in range(groups)]
    spread = lambda value: jnp.broadcast_to(value, (8, TILE))
    for j in range(0, TILE, at_once):
        g, t = divmod(j, 8)
        ks = range(at_once)
        rows = [spread(left[g][t + k : t + k + 1, :]) for k in ks]
        marks = [spread(right[g][t + k : t + k + 1, :]) for k in ks]
        p = {(k, m): spread(rows[k][:, j + m : j + m + 1]) for k in ks for m in range(k, at_once)}
        f, inv = {}, []
        for k in ks:
            inv.append(1.0 / p[k, k])
            for m in range(k + 1, at_once):
                f[m, k] = p[k, m] * inv[k]
            for m in range(k + 1, at_once):
                for n in range(m, at_once):
                    p[m, n] = p[m, n] - f[m, k] * p[k, n]
        for k in ks:
            for q in range(k):
                rows[k] = rows[k] - f[k, q] * rows[q]
                marks[k] = marks[k] - f[k, q] * marks[q]
        row_part, mark_part = [None] * at_once, [None] * at_once
        for k in reversed(ks):
            row_part[k] = rows[k] * inv[k]
            mark_part[k] = marks[k] * inv[k]
            for q in range(k + 1, at_once):
                row_part[k] = row_part[k] - f[q, k] * row_part[q]
                mark_part[k] = mark_part[k] - f[q, k] * mark_part[q]
        for i in range(g, groups):
            if i > g or t + at_once < 8:
                cols = [spread(left[i][:, j + k : j + k + 1]) for k in ks]
                if i == g:
                    cols = [jnp.where(sub >= t + at_once, col, 0.0) for col in cols]
                left_sum = (cols[0] * row_part[0] + cols[1] * row_part[1]) + (cols[2] * row_part[2] + cols[3] * row_part[3])
                right_sum = (cols[0] * mark_part[0] + cols[1] * mark_part[1]) + (cols[2] * mark_part[2] + cols[3] * mark_part[3])
                left[i] = left[i] - left_sum
                right[i] = right[i] - right_sum
        for k in ks:
            left[g] = jnp.where(sub == t + k, rows[k], left[g])
            right[g] = jnp.where(sub == t + k, marks[k], right[g])
    out = []
    for g in range(groups):
        diag = jnp.sum(jnp.where(lane == sub + 8 * g, left[g], 0.0), axis=1, keepdims=True)
        out.append(right[g] * (1.0 / jnp.sqrt(diag)))
    return jnp.concatenate(out, axis=0)


def eliminate_blocks(x_ref, first, last):
    def block(b, carry):
        at = pl.multiple_of(b * TILE, TILE)
        inverse = inverse_factor(x_ref[pl.ds(at, TILE), pl.ds(at, TILE)])
        solved = jnp.dot(inverse, x_ref[pl.ds(at, TILE), :], precision=lax.Precision.HIGHEST, preferred_element_type=jnp.float32)
        lanes = lax.broadcasted_iota(jnp.int32, (TILE, PANEL), 1)

        @pl.when(b < PANEL // TILE - 1)
        def _():
            coef = jnp.where(lanes >= at + TILE, solved[:, :PANEL], 0.0)
            x_ref[...] -= jnp.dot(coef.T, solved, precision=lax.Precision.HIGHEST, preferred_element_type=jnp.float32)

        x_ref[pl.ds(at, TILE), :] = solved
        return carry

    lax.fori_loop(first, last, block, 0)


def front_kernel(sample_count, shift_ref, feat_panel_ref, feat_ref, moment_panel_ref, x_ref):
    width = feat_ref.shape[1]
    start = 2 * PANEL
    panel_t = feat_panel_ref[...].T
    dot = functools.partial(jnp.dot, preferred_element_type=jnp.float32)
    rows = lax.broadcasted_iota(jnp.int32, (PANEL, PANEL), 0)
    cols = lax.broadcasted_iota(jnp.int32, (PANEL, PANEL), 1)
    eye = jnp.where(rows == cols, 1.0, 0.0)
    x_ref[:, 0:PANEL] = dot(panel_t, feat_panel_ref[...]) / sample_count + ridge * eye
    x_ref[:, PANEL:start] = eye
    rows = lax.broadcasted_iota(jnp.int32, (PANEL, width), 0)
    cols = lax.broadcasted_iota(jnp.int32, (PANEL, width), 1)
    own = jnp.where(rows == cols + shift_ref[0], ridge, 0.0)
    x_ref[:, start : start + width] = dot(panel_t, feat_ref[...]) / sample_count + own
    column = jnp.sum(eye * (moment_panel_ref[...] / sample_count), axis=1, keepdims=True)
    x_ref[:, start + width :] = jnp.broadcast_to(column, (PANEL, LANES))
    eliminate_blocks(x_ref, 0, PANEL // TILE // 2)


def back_kernel(sample_count, x_in_ref, moment_ref, inv_high_ref, inv_low_ref, cross_high_ref, cross_low_ref, reduced_ref, x_ref):
    width = moment_ref.shape[1]
    start = 2 * PANEL
    x_ref[...] = x_in_ref[...]
    eliminate_blocks(x_ref, PANEL // TILE // 2, PANEL // TILE)
    inv_high_ref[...], inv_low_ref[...] = split(x_ref[:, PANEL:start].T)
    cross = x_ref[:, start : start + width]
    cross_high_ref[...], cross_low_ref[...] = split(cross)
    solved = x_ref[:, start + width : start + width + 1]
    reduced = moment_ref[...] / sample_count - jnp.sum(cross * solved, axis=0, keepdims=True)
    reduced_ref[...] = jnp.sqrt(jnp.float32(sample_count)) * reduced


def eliminate_front(shift, feat_panel, feat, moment_panel):
    count, width = feat.shape
    vmem = pl.BlockSpec(memory_space=pltpu.VMEM)
    return pl.pallas_call(
        functools.partial(front_kernel, count),
        in_specs=[pl.BlockSpec(memory_space=pltpu.SMEM)] + [vmem] * 3,
        out_specs=vmem,
        out_shape=jax.ShapeDtypeStruct((PANEL, 2 * PANEL + width + LANES), jnp.float32),
        cost_estimate=pl.CostEstimate(flops=20 * 10**9, bytes_accessed=8 * 10**6, transcendentals=0),
        compiler_params=pltpu.CompilerParams(vmem_limit_bytes=VMEM_BYTES),
    )(shift, feat_panel, feat, moment_panel)


def eliminate_back(count, state, moment):
    width = moment.shape[1]
    vmem = pl.BlockSpec(memory_space=pltpu.VMEM)
    square = jax.ShapeDtypeStruct((PANEL, PANEL), jnp.bfloat16)
    wide = jax.ShapeDtypeStruct((PANEL, width), jnp.bfloat16)
    return pl.pallas_call(
        functools.partial(back_kernel, count),
        in_specs=[vmem] * 2,
        out_specs=[vmem] * 5,
        out_shape=[square, square, wide, wide, jax.ShapeDtypeStruct((1, width), jnp.float32)],
        scratch_shapes=[pltpu.VMEM(state.shape, jnp.float32)],
        cost_estimate=pl.CostEstimate(flops=20 * 10**9, bytes_accessed=8 * 10**6, transcendentals=0),
        compiler_params=pltpu.CompilerParams(vmem_limit_bytes=VMEM_BYTES),
    )(state, moment)


def three_pass(left, right_high, right_low):
    high, low = split(left)
    dot = functools.partial(jnp.dot, preferred_element_type=jnp.float32)
    return dot(high, right_high) + (dot(high, right_low) + dot(low, right_high))


def main_kernel(
    sample_count,
    blocks,
    order_ref,
    place_ref,
    pos_ref,
    *refs,
):
    freq_refs = refs[:blocks]
    (
        emb_ref,
        treated_ref,
        feat_ref,
        feat_panel_ref,
        inv_high_ref,
        inv_low_ref,
        cross_high_ref,
        cross_low_ref,
        schur_ref,
        panel_ref,
        slots,
        sems,
    ) = refs[blocks:]
    now = pl.program_id(0)

    def fetch(index, slot):
        for k in range(blocks):

            @pl.when(index == k)
            def _():
                pltpu.make_async_copy(freq_refs[k], slots.at[slot], sems.at[slot]).start()

    @pl.when(now == 0)
    def _():
        fetch(0, 0)

    fetch(now + 1, lax.rem(now + 1, 2))
    slot = lax.rem(now, 2)
    pltpu.make_async_copy(freq_refs[0], slots.at[slot], sems.at[slot]).wait()

    height = slots.shape[1]
    count, emb_width = emb_ref.shape
    width = feat_ref.shape[1]
    parts = slots[slot, :, emb_width : emb_width + LANES].astype(jnp.float32)
    base = (parts[:, 0:1] + parts[:, 1:2]) + parts[:, 2:3]
    full = (parts[:, 3:4] + parts[:, 4:5]) + parts[:, 5:6]
    own = jnp.zeros((height, width), jnp.float32)
    panel = jnp.zeros((height, PANEL), jnp.float32)
    step = count // pos_ref.shape[0]
    for j in range(count // step):
        at = j * step
        emb = emb_ref[pl.ds(pl.multiple_of(pos_ref[j] * step, step), step), :]
        scaled = lax.dot_general(
            slots[slot, :, :emb_width], emb, (((1,), (1,)), ((), ())), preferred_element_type=jnp.float32
        )
        phase = jnp.where(treated_ref[:, at : at + step] > 0.5, full, base)
        features = cosine_turns(scaled * turn + phase).astype(jnp.bfloat16)
        own += jnp.dot(features, feat_ref[at : at + step, :], preferred_element_type=jnp.float32)
        panel += jnp.dot(features, feat_panel_ref[at : at + step, :], preferred_element_type=jnp.float32)
    first = place_ref[0] + order_ref[now] * height
    rows = first + lax.broadcasted_iota(jnp.int32, (height, width), 0)
    cols = place_ref[1] + lax.broadcasted_iota(jnp.int32, (height, width), 1)
    own = own / sample_count + jnp.where(rows == cols, ridge, 0.0)
    rows = first + lax.broadcasted_iota(jnp.int32, (height, PANEL), 0)
    cols = place_ref[2] + lax.broadcasted_iota(jnp.int32, (height, PANEL), 1)
    panel = panel / sample_count + jnp.where(rows == cols, ridge, 0.0)
    factor = three_pass(panel, inv_high_ref[...], inv_low_ref[...])
    panel_ref[...] = factor
    schur_ref[...] = own - three_pass(factor, cross_high_ref[...], cross_low_ref[...])


def main(order, place, pos, freqs, emb, treated, feat, feat_panel, solved):
    blocks = len(freqs)
    height = freqs[0].shape[0]
    row_height = blocks * height
    emb_width = emb.shape[1]
    count, width = feat.shape
    fixed = lambda array: pl.BlockSpec(array.shape, lambda i, *_: (0, 0), pipeline_mode=pl.Buffered(1))
    moved = lambda cols: pl.BlockSpec((height, cols), lambda i, order, *_: (order[i], 0))
    flops = 2 * row_height * (count * (emb_width + width + PANEL) + 3 * PANEL * (PANEL + width))
    return pl.pallas_call(
        functools.partial(main_kernel, count, blocks),
        grid_spec=pltpu.PrefetchScalarGridSpec(
            num_scalar_prefetch=3,
            grid=(blocks,),
            in_specs=[pl.BlockSpec(memory_space=pl.ANY)] * blocks
            + [fixed(array) for array in (emb, treated, feat, feat_panel, *solved)],
            out_specs=[moved(width), moved(PANEL)],
            scratch_shapes=[
                pltpu.VMEM((2, height, freqs[0].shape[1]), jnp.bfloat16),
                pltpu.SemaphoreType.DMA((2,)),
            ],
        ),
        out_shape=[
            jax.ShapeDtypeStruct((row_height, width), jnp.float32),
            jax.ShapeDtypeStruct((row_height, PANEL), jnp.float32),
        ],
        cost_estimate=pl.CostEstimate(flops=flops, bytes_accessed=30 * 10**6, transcendentals=count * row_height),
        compiler_params=pltpu.CompilerParams(vmem_limit_bytes=VMEM_BYTES),
    )(order, place, pos, *freqs, emb, treated, feat, feat_panel, *solved)


def entry_kernel(
    axis_size, x_ref, freq_ref, emb_ref, out_ref, mine_ref, all_ref, sums, arrived, send_sems, recv_sems, local_sems
):
    samp, feat = lax.axis_index("samp"), lax.axis_index("feat")
    rows = x_ref.shape[0]
    bits = []
    while (1 << len(bits)) < axis_size:
        bits.append(1 << len(bits))
    sides = [(feat // bit) % 2 for bit in bits]
    mates = [feat + bit * (1 - 2 * side) for bit, side in zip(bits, sides)]

    barrier = pltpu.get_barrier_semaphore()
    for mate in mates:
        pl.semaphore_signal(barrier, inc=1, device_id=(samp, mate), device_id_type=pl.DeviceIdType.MESH)
    pl.semaphore_signal(barrier, inc=1, device_id=(1 - samp, feat), device_id_type=pl.DeviceIdType.MESH)
    pl.semaphore_wait(barrier, len(bits) + 1)

    def remote(source, target, device, index):
        return pltpu.make_async_remote_copy(
            src_ref=source,
            dst_ref=target,
            send_sem=send_sems.at[index],
            recv_sem=recv_sems.at[index],
            device_id=device,
            device_id_type=pl.DeviceIdType.MESH,
        )

    def send(source, target, mate, index):
        copy = remote(source, target, (samp, mate), index)
        copy.start()
        copy.wait()

    steps = 2 * len(bits)
    count = emb_ref.shape[0]
    part_rows = count // 2
    core = feat % 2
    mine_at = pl.multiple_of(samp * count + core * part_rows, 16)
    other_at = pl.multiple_of((1 - samp) * count + core * part_rows, 16)
    across = remote(
        emb_ref.at[pl.ds(pl.multiple_of(core * part_rows, 16), part_rows)],
        all_ref.at[pl.ds(mine_at, part_rows)],
        (1 - samp, feat),
        steps,
    )
    across.start()
    keeps = feat // (axis_size // 2) == samp
    crossing = remote(freq_ref, mine_ref, (samp, mates[-1]), steps + 1)
    keep = pltpu.make_async_copy(freq_ref, mine_ref, local_sems.at[0])
    stay = pltpu.make_async_copy(
        emb_ref, all_ref.at[pl.ds(pl.multiple_of(samp * count, 16), count)], local_sems.at[1]
    )

    stay.start()

    first = 0
    firsts = []
    size = rows
    source = x_ref
    landing = 0
    for index, (side, mate) in enumerate(zip(sides, mates)):
        size //= 2
        kept = pl.multiple_of(first + side * size, 16)
        given = pl.multiple_of(first + (1 - side) * size, 16)
        place = pl.ds(landing, size)
        send(source.at[pl.ds(given, size)], arrived.at[place], mate, index)
        total = source[pl.ds(kept, size), :] + arrived[place, :]
        landing += size
        first = kept
        firsts.append((first, size))
        if index < len(bits) - 1:
            sums[pl.ds(kept, size), :] = total
            source = sums
        else:
            out_ref[pl.ds(kept, size), :] = total
    for index in reversed(range(len(bits))):
        first, size = firsts[index]
        part = out_ref.at[pl.ds(first, size)]
        send(part, part, mates[index], len(bits) + index)
        if index == len(bits) - 1:

            @pl.when(keeps)
            def _():
                crossing.start()
                keep.start()

    across.wait()
    fetched = all_ref.at[pl.ds(other_at, part_rows)]
    forward = remote(fetched, fetched, (samp, mates[0]), steps + 2)
    forward.start()
    forward.wait()
    stay.wait()

    @pl.when(keeps)
    def _():
        crossing.wait_send()
        keep.wait()

    @pl.when(jnp.logical_not(keeps))
    def _():
        crossing.wait_recv()


def enter(x, freq_t, emb):
    axis_size = lax.axis_size("feat")
    steps = 2 * (axis_size.bit_length() - 1) + 3
    vmem, anywhere = pl.BlockSpec(memory_space=pltpu.VMEM), pl.BlockSpec(memory_space=pl.ANY)
    return pl.pallas_call(
        functools.partial(entry_kernel, axis_size),
        in_specs=[vmem, anywhere, anywhere],
        out_specs=[vmem, anywhere, anywhere],
        out_shape=[
            jax.ShapeDtypeStruct(x.shape, x.dtype),
            jax.ShapeDtypeStruct(freq_t.shape, freq_t.dtype),
            jax.ShapeDtypeStruct((2 * emb.shape[0], emb.shape[1]), emb.dtype),
        ],
        scratch_shapes=[
            pltpu.VMEM(x.shape, x.dtype),
            pltpu.VMEM(x.shape, x.dtype),
            pltpu.SemaphoreType.DMA((steps,)),
            pltpu.SemaphoreType.DMA((steps,)),
            pltpu.SemaphoreType.DMA((2,)),
        ],
        cost_estimate=pl.CostEstimate(flops=45 * 10**9, bytes_accessed=2 * 10**6, transcendentals=0),
        compiler_params=pltpu.CompilerParams(collective_id=0, has_side_effects=True, vmem_limit_bytes=16 * 1024 * 1024),
    )(x, freq_t, emb)


def swap(value, bits):
    return lax.ppermute(value, "feat", [(f, f ^ bits) for f in range(lax.axis_size("feat"))])


def per_device(embeddings, frequencies, phases, treat_freq, treatment, flips, panel):
    samp_size = lax.axis_size("samp")
    feat_size = lax.axis_size("feat")
    samp_index = lax.axis_index("samp")
    feat_index = lax.axis_index("feat")
    emb_width, col_width = frequencies.shape
    feat_total = col_width * feat_size
    row_height = feat_total // samp_size
    first_col = panel[0] * PANEL
    first_dev = first_col // col_width
    staged = samp_size == 2 and feat_size == 16 and col_width == PANEL
    half = 8

    base = phases * turn
    parts = jnp.stack(thirds(base) + thirds(base + treat_freq * turn))
    freq_t = jnp.concatenate([frequencies.T, jnp.pad(parts.T, ((0, 0), (0, LANES - 6)))], axis=1)

    treated = treatment.astype(jnp.float32)
    flipped = flips.astype(jnp.float32)
    counter = treated + flipped - 2.0 * treated * flipped
    marks = jnp.stack([treated, counter])
    if staged:
        masked = jnp.where(feat_index == first_dev, freq_t, jnp.zeros_like(freq_t))
        other_marks = lax.ppermute(marks, "samp", [(0, 1), (1, 0)])
        first = samp_index == 0
        marks = jnp.concatenate([jnp.where(first, marks, other_marks), jnp.where(first, other_marks, marks)], axis=1)
        panel_freq, mine, emb = enter(masked, freq_t, embeddings)
        near = [swap(mine, 4), swap(mine, 2), swap(mine, 6)]
    else:
        emb = lax.all_gather(embeddings, "samp", axis=0, tiled=True)
        marks = lax.all_gather(marks, "samp", axis=1, tiled=True)
        panel_freq = []
        for member in range(PANEL // col_width):
            own = feat_index == first_dev + member
            panel_freq.append(lax.psum(jnp.where(own, freq_t, jnp.zeros_like(freq_t)), "feat"))
        panel_freq = jnp.concatenate(panel_freq, axis=0)
    pos = jnp.arange(emb.shape[0] // 512, dtype=jnp.int32)

    treated_col, counter_col = marks[0][:, None], marks[1][:, None]
    feat, moment = make_features(pos, emb, freq_t, treated_col, counter_col)
    feat_panel, moment_panel = make_features(pos, emb, panel_freq, treated_col, counter_col)
    own_col = feat_index * col_width
    shift = (own_col - first_col).reshape(1).astype(jnp.int32)
    state = eliminate_front(shift, feat_panel, feat, moment_panel)
    if staged:
        state, near = lax.optimization_barrier((state, near))
        near = [mine] + near
        freqs = near + [swap(block, 1) for block in near]
        order = jnp.bitwise_xor(feat_index % half, jnp.array([0, 4, 2, 6, 1, 5, 3, 7], jnp.int32))
    else:
        rows = lax.all_gather(freq_t, "feat", axis=0, tiled=True)
        rows = lax.dynamic_slice_in_dim(rows, samp_index * row_height, row_height, 0)
        freqs = jnp.split(rows, row_height // col_width, axis=0)
        order = jnp.arange(row_height // col_width, dtype=jnp.int32)
    *solved, reduced = eliminate_back(emb.shape[0], state, moment)
    place = jnp.stack([samp_index * row_height, own_col, first_col]).astype(jnp.int32)
    schur, panel_factor = main(order, place, pos, freqs, emb, marks[:1], feat, feat_panel, solved)
    return schur, panel_factor, reduced[0]


def solution(mesh):
    return jax.shard_map(
        per_device,
        mesh=mesh,
        in_specs=(
            P("samp", None),
            P(None, "feat"),
            P("feat"),
            P("feat"),
            P("samp"),
            P("samp"),
            P(),
        ),
        out_specs=(P("samp", "feat"), P("samp", None), P("feat")),
        check_vma=False,
    )
```
